512 devices in a mesh: section: 4 (over x), dom: 128 (over z, y, core).
Axes of the slice: x: 4, y: 4, z: 16, core: 2. Of those that a mesh axis runs over, the one named last changes fastest.
Arguments:
- latent: bfloat16 [4, 16384, 512], P(None, 'dom'), may hold values from -32 to 32
- cotangent: bfloat16 [4, 16384, 512], P(None, 'dom'), may hold values from -6 to 6
- source_weight: bfloat16 [4, 512, 512], P('section'), may hold values from -0.25 to 0.25
- self_weight: bfloat16 [4, 512, 512], P('section'), may hold values from -0.25 to 0.25
- out_weight: bfloat16 [4, 512, 512], P('section'), may hold values from -0.25 to 0.25
- norm_gain: float32 [4, 512], P('section'), may hold values from 0.1 to 1.9
- edge_tiles: bfloat16 [512, 128, 128], P('dom'), may hold values from -0.4 to 0.4
- pair_source: int32 [512], P('dom'), may hold values from 0 to 127, as said below
- live_pairs: int32 [128], P('dom'), may hold values from 1 to 4, as said below
Outputs:
- layer_latents: bfloat16 [4, 4, 16384, 512], P('section', None, 'dom')
- layer_grads: bfloat16 [4, 4, 16384, 512], P('section', None, 'dom')
The draws below stay inside these ranges and needn't reach their ends.
Inputs may be any that keep to these rules, and one draw needn't show every extreme that they name: `pair_source`: the sending block of every slot of partition d, live or not, is owned by a partition from d - 2 to d + 2. `live_pairs`: some partition has all 4 slots live.
All inputs are finite; a program needn't handle non-finite values.
Results may differ from the reference program's by a relative error of at most 0.025.
Values may be sent and summed in bfloat16 or wider, within the bound.
No kernel may reach another device: no remote copies, remote signals or barrier semaphores. Data moves between devices by JAX's collectives and lax.ppermute only.
A program may use at most 64 MiB of HBM per device.

```python
import jax
import jax.numpy as jnp
from jax import lax

H = 512
BLOCK = 128
BLOCKS_DEV = 1
MEMBERS = 4
WIN = 2
LAYERS = 4
PAIRS_DEV = 4
NODES = 16384
PAIRS = 512
N_DOM = 128


def draw_latent(key, part):
    key = jax.random.fold_in(key, 11)
    keys = jax.random.split(key, 5)
    row_scale = jnp.exp(jax.random.uniform(keys[0], (MEMBERS, NODES, 1), jnp.float32, jnp.log(0.4), jnp.log(4.0)))
    column_scale = jnp.exp(jax.random.uniform(keys[1], (1, 1, H), jnp.float32, jnp.log(0.5), jnp.log(2.0)))
    base = jax.random.truncated_normal(keys[4], -4.0, 4.0, (MEMBERS, NODES, H), jnp.float32)
    return (base * row_scale * column_scale).astype(jnp.bfloat16)


def draw_edge_tiles(key, part):
    key = jax.random.fold_in(key, 23)
    keys = jax.random.split(key, 3)
    present = jax.random.bernoulli(keys[0], 0.5, (PAIRS, BLOCK, BLOCK))
    weights = 0.1 * jax.random.truncated_normal(keys[2], -3.9, 3.9, (PAIRS, BLOCK, BLOCK), jnp.float32)
    return jnp.where(present, weights, 0.0).astype(jnp.bfloat16)


def draw_pair_source(key, part):
    key = jax.random.fold_in(key, 37)
    keys = jax.random.split(key, 2)
    slot_total = N_DOM * PAIRS_DEV
    owner = jnp.arange(slot_total, dtype=jnp.int32) // PAIRS_DEV
    hop_offset = jax.random.randint(keys[0], (slot_total,), -WIN, WIN + 1, dtype=jnp.int32)
    inner_block = jax.random.randint(keys[1], (slot_total,), 0, BLOCKS_DEV, dtype=jnp.int32)
    partner = jnp.clip(owner + hop_offset, 0, N_DOM - 1)
    chosen = partner * BLOCKS_DEV + inner_block
    chosen = chosen.at[0].set(0)
    chosen = chosen.at[slot_total - 1].set(N_DOM * BLOCKS_DEV - 1)
    return chosen.astype(jnp.int32)


def draw_live_pairs(key, part):
    key = jax.random.fold_in(key, 53)
    keys = jax.random.split(key, 3)
    first_draw = jax.random.randint(keys[0], (N_DOM,), 1, PAIRS_DEV + 1, dtype=jnp.int32)
    second_draw = jax.random.randint(keys[1], (N_DOM,), 1, PAIRS_DEV + 1, dtype=jnp.int32)
    counts = jnp.minimum(first_draw, second_draw)
    busiest = jax.random.randint(keys[2], (), 0, N_DOM, dtype=jnp.int32)
    positions = jnp.arange(N_DOM, dtype=jnp.int32)
    counts = jnp.where(positions == busiest, PAIRS_DEV, counts)
    counts = jnp.where(positions == (busiest + 1) % N_DOM, 1, counts)
    return counts.astype(jnp.int32)


def shard_levels(own_key, extent, cuts, least, top_value):
    loudness, own = 1.0, jax.random.fold_in(own_key, 6)
    for position, parts in cuts:
        heights = jnp.exp(jax.random.uniform(jax.random.fold_in(own, position), (parts,), jnp.float32, least / len(cuts), top_value / len(cuts)))
        loudness = loudness * jnp.repeat(heights, extent[position] // parts).reshape([-1 if axis == position else 1 for axis in range(len(extent))])
    return loudness


def gaussian(key, extent, width, most, pieces=(), held_as=jnp.bfloat16):
    values = jax.random.normal(key, extent, jnp.float32) * width
    if len(pieces) > 0:
        values = shard_levels(key, extent, pieces, -0.22, 0.18) * values
    return jnp.clip(values, min=-most, max=most).astype(held_as)


def setup_inputs(seed: int = 0) -> dict:
    arg_keys = jax.random.split(jax.random.key(seed), 10)
    latent = draw_latent(jax.random.fold_in(arg_keys[9], 71), 0)
    cotangent = gaussian(arg_keys[1], (MEMBERS, NODES, H), 1.0, 6.0, ((1, 128),))
    source_weight = gaussian(arg_keys[2], (LAYERS, H, H), H ** -0.5, 0.25, ((0, 4),))
    self_weight = gaussian(arg_keys[3], (LAYERS, H, H), H ** -0.5, 0.25, ((0, 4),))
    out_weight = gaussian(arg_keys[4], (LAYERS, H, H), H ** -0.5, 0.25, ((0, 4),))
    norm_gain = jnp.clip(1.0 + 0.18 * jax.random.normal(arg_keys[5], (LAYERS, H), jnp.float32), 0.1, 1.9)
    edge_tiles = draw_edge_tiles(jax.random.fold_in(arg_keys[9], 71), 0)
    pair_source = draw_pair_source(jax.random.fold_in(arg_keys[9], 71), 0)
    live_pairs = draw_live_pairs(jax.random.fold_in(arg_keys[9], 71), 0)
    return dict(latent=latent, cotangent=cotangent, source_weight=source_weight, self_weight=self_weight, out_weight=out_weight, norm_gain=norm_gain, edge_tiles=edge_tiles, pair_source=pair_source, live_pairs=live_pairs)


EPS = 1e-05

def norm_rows(values, layer_gain):
    widened = values.astype(jnp.float32)
    centre = widened - lax.optimization_barrier(jnp.mean(widened, axis=-1, keepdims=True))
    inv_scale = lax.rsqrt(lax.optimization_barrier(jnp.mean(centre * centre, axis=-1, keepdims=True)) + EPS)
    normed = centre * inv_scale
    return (normed, inv_scale, (normed * layer_gain).astype(jnp.bfloat16))

def pair_matrix(edge_tiles, live_count, blocks):
    slots, block_rows, _ = edge_tiles.shape
    slot_order = jnp.arange(slots, dtype=jnp.int32)
    target = slot_order * blocks // live_count
    select = (target[None, :] == jnp.arange(blocks, dtype=jnp.int32)[:, None]) & (slot_order < live_count)[None, :]
    spread = jnp.transpose(edge_tiles, (1, 0, 2))
    masked = jnp.where(select[:, None, :, None], spread[None], jnp.zeros((), edge_tiles.dtype))
    return masked.reshape(blocks * block_rows, slots * block_rows)

def one_sample(latent, cotangent, source_weight, self_weight, out_weight, norm_gain, edge_tiles, pair_source, live_pairs):
    blocks_all = N_DOM * BLOCKS_DEV
    window_blocks = (2 * WIN + 1) * BLOCKS_DEV
    tile_sets = edge_tiles.reshape(N_DOM, PAIRS_DEV, BLOCK, BLOCK)
    source_sets = pair_source.reshape(N_DOM, PAIRS_DEV)
    part_numbers = jnp.arange(N_DOM, dtype=jnp.int32)
    values = latent
    saved = []
    latents_out = []
    for layer in range(LAYERS):
        normed, inv_scale, unit = norm_rows(values, norm_gain[layer])
        source = jnp.dot(unit, source_weight[layer], preferred_element_type=jnp.float32).astype(jnp.bfloat16)
        source_blocks = source.reshape(blocks_all, BLOCK, H)

        def aggregate(item):
            tile_set, source_set, live_count = item
            matrix = pair_matrix(tile_set, live_count, BLOCKS_DEV)
            picked = source_blocks[source_set].reshape(PAIRS_DEV * BLOCK, H)
            return jnp.dot(matrix, picked, preferred_element_type=jnp.float32)
        gathered = lax.map(aggregate, (tile_sets, source_sets, live_pairs)).reshape(NODES, H)
        pre_act = gathered + jnp.dot(unit, self_weight[layer], preferred_element_type=jnp.float32)
        activation = jax.nn.silu(pre_act).astype(jnp.bfloat16)
        values = (values.astype(jnp.float32) + jnp.dot(activation, out_weight[layer], preferred_element_type=jnp.float32)).astype(jnp.bfloat16)
        saved.append((normed, inv_scale, pre_act))
        latents_out.append(values)
    gradient = cotangent
    grads_out = [None] * LAYERS
    for layer in range(LAYERS - 1, -1, -1):
        normed, inv_scale, pre_act = saved[layer]
        grad_activation = jnp.dot(gradient, out_weight[layer].T, preferred_element_type=jnp.float32)
        sigma = jax.nn.sigmoid(pre_act)
        grad_pre = (grad_activation * sigma * (1.0 + pre_act * (1.0 - sigma))).astype(jnp.bfloat16)
        grad_parts = grad_pre.reshape(N_DOM, BLOCKS_DEV * BLOCK, H)

        def spread_back(carry, item):
            tile_set, source_set, live_count, part_index, grad_part = item
            matrix = pair_matrix(tile_set, live_count, BLOCKS_DEV)
            contributions = jnp.dot(matrix.T, grad_part, preferred_element_type=jnp.float32).reshape(PAIRS_DEV, BLOCK, H)
            slot_in_window = (source_set - (part_index - WIN) * BLOCKS_DEV).astype(jnp.int32)
            per_slot = jax.ops.segment_sum(contributions, slot_in_window, num_segments=window_blocks)
            rounded = lax.optimization_barrier(per_slot.astype(jnp.bfloat16)).astype(jnp.float32)
            start_block = (part_index * BLOCKS_DEV).astype(jnp.int32)
            current = lax.dynamic_slice_in_dim(carry, start_block, window_blocks, 0)
            return (lax.dynamic_update_slice_in_dim(carry, current + rounded, start_block, 0), None)
        padded = jnp.zeros(((N_DOM + 2 * WIN) * BLOCKS_DEV, BLOCK, H), jnp.float32)
        padded, _ = lax.scan(spread_back, padded, (tile_sets, source_sets, live_pairs, part_numbers, grad_parts))
        back = padded[WIN * BLOCKS_DEV:WIN * BLOCKS_DEV + blocks_all].reshape(NODES, H).astype(jnp.bfloat16)
        grad_unit = jnp.dot(grad_pre, self_weight[layer].T, preferred_element_type=jnp.float32)
        grad_unit = grad_unit + jnp.dot(back, source_weight[layer].T, preferred_element_type=jnp.float32)
        grad_normed = grad_unit * norm_gain[layer]
        grad_in = inv_scale * (grad_normed - lax.optimization_barrier(jnp.mean(grad_normed, axis=-1, keepdims=True)) - normed * lax.optimization_barrier(jnp.mean(grad_normed * normed, axis=-1, keepdims=True)))
        gradient = (gradient.astype(jnp.float32) + grad_in).astype(jnp.bfloat16)
        grads_out[layer] = gradient
    return (jnp.stack(latents_out), jnp.stack(grads_out))

def reference(latent, cotangent, source_weight, self_weight, out_weight, norm_gain, edge_tiles, pair_source, live_pairs):
    latent_list = []
    grad_list = []
    for member in range(MEMBERS):
        lat, grd = one_sample(latent[member], cotangent[member], source_weight, self_weight, out_weight, norm_gain, edge_tiles, pair_source, live_pairs)
        latent_list.append(lat)
        grad_list.append(grd)
    return (jnp.stack(latent_list, axis=1), jnp.stack(grad_list, axis=1))
```

```python
import functools

import jax
import jax.numpy as jnp
import numpy as np
from jax import lax
from jax.experimental import pallas as pl
from jax.experimental.pallas import tpu as pltpu
from jax.sharding import Mesh, PartitionSpec as P

EPS = 1e-05
H = 512
B = 128
PAIR = 2 * B
BAND = 3 * PAIR
REACH = 4
W_ROWS = 3 * H + 32
W_HALF = W_ROWS // 2
F32, BF16 = jnp.float32, jnp.bfloat16
VMEM = pl.BlockSpec(memory_space=pltpu.VMEM)
SMEM = pl.BlockSpec(memory_space=pltpu.SMEM)


def rows(index, size=PAIR):
    if isinstance(index, int):
        return pl.ds(index * size, size)
    return pl.ds(pl.multiple_of(index * size, size), size)


def dot(a, b):
    return jnp.dot(a, b, preferred_element_type=F32)


def dot_t(a, b):
    return lax.dot_general(a, b, (((1,), (1,)), ((), ())), preferred_element_type=F32)


def normed_rows(values):
    wide = values.astype(F32)
    centre = wide - jnp.mean(wide, axis=-1, keepdims=True)
    inv = lax.rsqrt(jnp.mean(centre * centre, axis=-1, keepdims=True) + EPS)
    return centre * inv, inv


def call(kernel, outs, specs, scratch, limit_mib, name, flops=0):
    return pl.pallas_call(
        kernel,
        out_shape=[jax.ShapeDtypeStruct(s, d) for s, d in outs],
        in_specs=specs,
        out_specs=[VMEM] * len(outs),
        scratch_shapes=scratch,
        compiler_params=pltpu.CompilerParams(vmem_limit_bytes=limit_mib << 20),
        name=name,
    )


def prepare_kernel(ids, source, live, latent, cotangent, w_a, w_b, w_c, gain, tiles, own, weights):
    sample = ids[0]
    own[:, 0:H] = latent[sample]
    own[:, H + BAND :] = cotangent[sample]
    slots = tiles.shape[0]
    base = 2 * (ids[2] - 1)
    for column in range(6):
        total = jnp.zeros((B, B), F32)
        for slot in range(slots):
            hit = (source[slot] - base == column) & (slot < live[0])
            total = total + jnp.where(hit, tiles[slot].astype(F32), 0.0)
        own[:, H + column * B : H + (column + 1) * B] = total.astype(BF16)
    weights[0:H, :] = w_a[0]
    weights[H : 2 * H, :] = w_b[0]
    weights[2 * H : 3 * H, :] = w_c[0]
    rest = jnp.broadcast_to(gain[0:1, :], (16, H))
    high = rest.astype(BF16).astype(F32)
    rest = rest - high
    mid = rest.astype(BF16).astype(F32)
    low = rest - mid
    row = lax.broadcasted_iota(jnp.int32, (16, H), 0)
    terms = jnp.where(row == 0, high, jnp.where(row == 1, mid, jnp.where(row == 2, low, 0.0)))
    weights[3 * H : 3 * H + 16, :] = terms.astype(BF16)
    weights[3 * H + 16 : 3 * H + 32, :] = jnp.zeros((16, H), BF16)


def layer_gain(weights, layer):
    terms = weights[layer * W_ROWS + 3 * H : layer * W_ROWS + 3 * H + 16, :].astype(F32)
    return jnp.sum(terms, axis=0, keepdims=True)


def weight(weights, layer, which):
    start = layer * W_ROWS + which * H
    return weights[start : start + H, :]


def forward_kernel(
    ids, own, m1, m2, m3, m4, t1, t2, t3, t4, w_own, w_m, w_t, w_mh, w_th,
    latents, grad_pre, turned, v3_out, v2_out, v1_out, v0_out, f2_out, f1_out, f0_out, weights,
    v_a, v_b, band, unit, source,
):
    section, core = ids[0], ids[1]
    weights[pl.ds(pl.multiple_of(section * W_ROWS, 16), W_ROWS), :] = w_own[...]
    before, after = (section + 3) % 4, (section + 1) % 4
    mine = jnp.where(core == 0, before, after)
    theirs = jnp.where(core == 0, after, before)
    far = (section + 2) % 4
    weights[pl.ds(pl.multiple_of(mine * W_ROWS, 16), W_ROWS), :] = w_m[...]
    weights[pl.ds(pl.multiple_of(theirs * W_ROWS, 16), W_ROWS), :] = w_t[...]
    weights[pl.ds(pl.multiple_of(far * W_ROWS + core * W_HALF, 16), W_HALF), :] = w_mh[...]
    weights[pl.ds(pl.multiple_of(far * W_ROWS + (1 - core) * W_HALF, 16), W_HALF), :] = w_th[...]

    v_a[rows(REACH), :] = own[:, 0:H]
    band[rows(REACH - 1), :] = own[:, H : H + BAND]
    for step, (m, t) in enumerate(((m1, t1), (m2, t2), (m3, t3), (m4, t4)), start=1):
        at_m = REACH - step + 2 * step * core
        at_t = 2 * REACH - at_m
        v_a[rows(at_m), :] = m[:, 0:H]
        v_a[rows(at_t), :] = t[:, 0:H]
        if step < REACH:
            band[rows(at_m - 1), :] = m[:, H : H + BAND]
            band[rows(at_t - 1), :] = t[:, H : H + BAND]

    mine_rows = rows(core, B)
    v0_out[...] = own[:, 0:H]
    now, later = v_a, v_b
    for layer in range(4):
        low, high = layer, 2 * REACH - layer
        gain = layer_gain(weights, layer)

        def project(j):
            value, _ = normed_rows(now[rows(j), :])
            held = (value * gain).astype(BF16)
            unit[rows(j), :] = held
            source[rows(j), :] = dot(held, weight(weights, layer, 0)).astype(BF16)

        def update(j):
            window = source[pl.ds(pl.multiple_of((j - 1) * PAIR, PAIR), BAND), :]
            pre = dot(band[rows(j - 1), :], window)
            pre = pre + dot(unit[rows(j), :], weight(weights, layer, 1))
            sigma = 1.0 / (1.0 + jnp.exp(-pre))
            act = (pre * sigma).astype(BF16)
            value = now[rows(j), :].astype(F32) + dot(act, weight(weights, layer, 2))
            later[rows(j), :] = value.astype(BF16)
            return sigma * (1.0 + pre * (1.0 - sigma))

        def step(j, carry):
            factor = update(j)
            if layer == 1:
                f1_out[rows(j - 2), :] = factor
            if layer in (0, 2):
                out = f0_out if layer == 0 else f2_out
                if layer == 2:
                    out[rows(j - 3), :] = factor
                else:
                    @pl.when((j >= 3) & (j <= 5))
                    def _():
                        out[rows(j - 3), :] = factor
            project(j + 2)
            return carry

        def first(j, carry):
            project(j)
            return carry

        lax.fori_loop(low, low + 3, first, 0)
        if layer < 3:
            lax.fori_loop(low + 1, high - 1, step, 0)
            factor = update(high - 1)
            if layer == 1:
                f1_out[rows(high - 3), :] = factor
            if layer == 2:
                f2_out[rows(high - 4), :] = factor
        else:
            factor = update(REACH)
            incoming = dot_t(own[:, H + BAND :], weight(weights, 3, 2))
            grad_pre[...] = (incoming * factor).astype(BF16)
        latents[layer] = later[pl.ds(pl.multiple_of(REACH * PAIR + core * B, B), B), :]
        if layer == 0:
            v1_out[...] = later[3 * PAIR : 6 * PAIR, :]
        if layer == 1:
            v2_out[...] = later[4 * PAIR : 5 * PAIR, :]
        if layer == 2:
            v3_out[...] = later[3 * PAIR : 6 * PAIR, :]
        now, later = later, now

    for j in range(3, 6):
        for i in range(j - 1, j + 2):
            column = (j - i + 1) * PAIR
            piece = band[(i - 1) * PAIR : i * PAIR, column : column + PAIR]
            turned[(j - 3) * PAIR : (j - 2) * PAIR, (i - j + 1) * PAIR : (i - j + 2) * PAIR] = (
                piece.astype(F32).T.astype(BF16)
            )


def grad_pair(gradient, grad_pre, window, turned, values, weights, layer):
    back = dot(turned, window).astype(BF16)
    grad_unit = dot_t(grad_pre, weight(weights, layer, 1))
    grad_unit = grad_unit + dot_t(back, weight(weights, layer, 0))
    normed, inv = normed_rows(values)
    e = grad_unit * layer_gain(weights, layer)
    grad_in = inv * (
        e
        - jnp.mean(e, axis=-1, keepdims=True)
        - normed * jnp.mean(e * normed, axis=-1, keepdims=True)
    )
    return (gradient.astype(F32) + grad_in).astype(BF16)


def place(target, own, received, other, core, steps, offset):
    target[rows(offset), :] = own
    for step in range(1, steps + 1):
        at_m = offset - step + 2 * step * core
        at_t = 2 * offset - at_m
        target[rows(at_m), :] = received[(step - 1) * PAIR : step * PAIR, :]
        target[rows(at_t), :] = other[(step - 1) * PAIR : step * PAIR, :]


def backward_a_kernel(
    ids, grad_pre, received, other, own, m1, t1, turned, v3, v2, f2, weights,
    g3_out, g2_out, held, cot, g3, gp2,
):
    core = ids[1]
    place(held, grad_pre[...], received, other, core, 2, 2)
    cot[rows(1), :] = own[...]
    cot[rows(2 * core), :] = m1[...]
    cot[rows(2 - 2 * core), :] = t1[...]
    for j in range(3):
        g3[rows(j), :] = grad_pair(
            cot[rows(j), :], held[rows(j + 1), :], held[j * PAIR : j * PAIR + BAND, :],
            turned[rows(j), :], v3[rows(j), :], weights, 3,
        )
        gp2[rows(j), :] = (dot_t(g3[rows(j), :], weight(weights, 2, 2)) * f2[rows(j), :]).astype(BF16)
    g3_out[...] = g3[pl.ds(pl.multiple_of(PAIR + core * B, B), B), :]
    g2_out[...] = grad_pair(
        g3[rows(1), :], gp2[rows(1), :], gp2[...], turned[rows(1), :], v2[...], weights, 2
    )


def backward_b_kernel(
    ids, g2_own, received, other, turned, v1, v0, f1, f0, weights,
    g1_out, g0_out, g2, gp1, g1, gp0,
):
    core = ids[1]
    place(g2, g2_own[...], received, other, core, 2, 2)
    for j in range(5):
        gp1[rows(j), :] = (dot_t(g2[rows(j), :], weight(weights, 1, 2)) * f1[rows(j), :]).astype(BF16)
    for j in range(3):
        g1[rows(j), :] = grad_pair(
            g2[rows(j + 1), :], gp1[rows(j + 1), :], gp1[j * PAIR : j * PAIR + BAND, :],
            turned[rows(j), :], v1[rows(j), :], weights, 1,
        )
        gp0[rows(j), :] = (dot_t(g1[rows(j), :], weight(weights, 0, 2)) * f0[rows(j), :]).astype(BF16)
    g1_out[...] = g1[pl.ds(pl.multiple_of(PAIR + core * B, B), B), :]
    g0 = grad_pair(g1[rows(1), :], gp0[rows(1), :], gp0[...], turned[rows(1), :], v0[...], weights, 0)
    g1[rows(0), :] = g0
    g0_out[...] = g1[rows(core, B), :]


def swap(value):
    return lax.ppermute(value, "core", [(0, 1), (1, 0)])


def spread(value, steps):
    chips = lax.axis_size("chip")
    pairs = []
    for c in range(chips):
        if c + steps < chips:
            pairs.append((2 * c, 2 * (c + steps)))
        if c - steps >= 0:
            pairs.append((2 * c + 1, 2 * (c - steps) + 1))
    return lax.ppermute(value, ("chip", "core"), pairs)


def around(value):
    count = lax.axis_size("section")
    pairs = []
    for s in range(count):
        pairs.append((2 * s, 2 * ((s + 1) % count)))
        pairs.append((2 * s + 1, 2 * ((s - 1) % count) + 1))
    return lax.ppermute(value, ("section", "core"), pairs)


def to_layers(stacked, section):
    count = stacked.shape[0]
    out = jnp.zeros_like(stacked)
    keep = lax.dynamic_index_in_dim(stacked, section, 0, keepdims=True)
    out = lax.dynamic_update_slice_in_dim(out, keep, section, 0)
    for step in range(1, count):
        piece = lax.dynamic_index_in_dim(stacked, (section + step) % count, 0, keepdims=True)
        got = lax.ppermute(piece, "section", [(s, (s + step) % count) for s in range(count)])
        out = lax.dynamic_update_slice_in_dim(out, got, (section - step) % count, 0)
    return out


def body(latent, cotangent, w_a, w_b, w_c, gain, tiles, pair_source, live_pairs):
    section, core, chip = lax.axis_index("section"), lax.axis_index("core"), lax.axis_index("chip")
    ids = jnp.stack([section, core, chip]).astype(jnp.int32)
    wide = H + BAND

    own, w_own = call(
        prepare_kernel,
        [((B, wide + H), BF16), ((W_ROWS, H), BF16)],
        [SMEM, SMEM, SMEM] + [VMEM] * 7,
        [],
        32,
        "prepare",
    )(ids, pair_source, live_pairs, latent, cotangent, w_a, w_b, w_c, gain, tiles)

    w_m = around(w_own)
    partner = swap(own)
    first = jnp.where(core == 0, own, partner)
    second = jnp.where(core == 0, partner, own)
    pair = jnp.concatenate([first, second], axis=0)
    m1 = spread(pair, 1)
    near = pair[:, :wide]
    m2, m3 = spread(near, 2), spread(near, 3)
    m4 = spread(pair[:, :H], 4)
    w_mh = around(lax.dynamic_slice_in_dim(w_m, core * W_HALF, W_HALF, 0))
    w_t, w_th = swap(w_m), swap(w_mh)
    t1, t2, t3, t4 = swap(m1), swap(m2), swap(m3), swap(m4)

    span = 2 * REACH + 1
    latents, grad_pre, turned, v3, v2, v1, v0, f2, f1, f0, weights = call(
        forward_kernel,
        [
            ((4, B, H), BF16), ((PAIR, H), BF16), ((3 * PAIR, BAND), BF16),
            ((3 * PAIR, H), BF16), ((PAIR, H), BF16), ((3 * PAIR, H), BF16), ((PAIR, H), BF16),
            ((3 * PAIR, H), F32), ((5 * PAIR, H), F32), ((3 * PAIR, H), F32),
            ((4 * W_ROWS, H), BF16),
        ],
        [SMEM] + [VMEM] * 14,
        [
            pltpu.VMEM((span * PAIR, H), BF16), pltpu.VMEM((span * PAIR, H), BF16),
            pltpu.VMEM(((span - 2) * PAIR, BAND), BF16),
            pltpu.VMEM((span * PAIR, H), BF16), pltpu.VMEM((span * PAIR, H), BF16),
        ],
        56,
        "forward",
    )(ids, pair, m1, m2, m3, m4, t1, t2, t3, t4, w_own, w_m, w_t, w_mh, w_th)

    received = jnp.concatenate([spread(grad_pre, 1), spread(grad_pre, 2)], axis=0)
    other = swap(received)
    g3, g2 = call(
        backward_a_kernel,
        [((B, H), BF16), ((PAIR, H), BF16)],
        [SMEM] + [VMEM] * 11,
        [
            pltpu.VMEM((5 * PAIR, H), BF16), pltpu.VMEM((3 * PAIR, H), BF16),
            pltpu.VMEM((3 * PAIR, H), BF16), pltpu.VMEM((3 * PAIR, H), BF16),
        ],
        40,
        "backward_a",
    )(ids, grad_pre, received, other, pair[:, wide:], m1[:, wide:], t1[:, wide:], turned, v3, v2, f2, weights)

    latent_result = to_layers(latents, section)

    received = jnp.concatenate([spread(g2, 1), spread(g2, 2)], axis=0)
    other = swap(received)
    g1, g0 = call(
        backward_b_kernel,
        [((B, H), BF16), ((B, H), BF16)],
        [SMEM] + [VMEM] * 9,
        [
            pltpu.VMEM((5 * PAIR, H), BF16), pltpu.VMEM((5 * PAIR, H), BF16),
            pltpu.VMEM((3 * PAIR, H), BF16), pltpu.VMEM((3 * PAIR, H), BF16),
        ],
        40,
        "backward_b",
    )(ids, g2, received, other, turned, v1, v0, f1, f0, weights)

    g2_own = lax.dynamic_slice_in_dim(g2, core * B, B, 0)
    grad_result = to_layers(jnp.stack([g0, g1, g2_own, g3]), section)
    return (latent_result[None], grad_result[None])


def solution(mesh):
    devices = np.asarray(mesh.devices)
    sections, parts = devices.shape
    split = Mesh(devices.reshape(sections, parts // 2, 2), ("section", "chip", "core"))
    dom = ("chip", "core")
    in_specs = (
        P(None, dom, None),
        P(None, dom, None),
        P("section", None, None),
        P("section", None, None),
        P("section", None, None),
        P("section", None),
        P(dom, None, None),
        P(dom),
        P(dom),
    )
    out_specs = (P("section", None, dom, None), P("section", None, dom, None))
    return jax.shard_map(body, mesh=split, in_specs=in_specs, out_specs=out_specs, check_vma=False)
```

```python
import functools

import jax
import jax.numpy as jnp
import numpy as np
from jax import lax
from jax.experimental import pallas as pl
from jax.experimental.pallas import tpu as pltpu
from jax.sharding import Mesh, PartitionSpec as P

EPS = 1e-05
H = 512
B = 128
PAIR = 2 * B
BAND = 3 * PAIR
REACH = 4
W_ROWS = 3 * H + 32
W_HALF = W_ROWS // 2
F32, BF16 = jnp.float32, jnp.bfloat16
VMEM = pl.BlockSpec(memory_space=pltpu.VMEM)
HBM = pl.BlockSpec(memory_space=pltpu.HBM)
FWD_MIB, BWD_MIB = 24, 12


def rows(index, size=PAIR):
    if isinstance(index, int):
        return pl.ds(index * size, size)
    return pl.ds(pl.multiple_of(index * size, size), size)


def dot(a, b):
    return jnp.dot(a, b, preferred_element_type=F32)


def dot_t(a, b):
    return lax.dot_general(a, b, (((1,), (1,)), ((), ())), preferred_element_type=F32)


def normed_rows(values):
    wide = values.astype(F32)
    centre = wide - jnp.mean(wide, axis=-1, keepdims=True)
    inv = lax.rsqrt(jnp.mean(centre * centre, axis=-1, keepdims=True) + EPS)
    return centre * inv, inv


def call(kernel, outs, specs, scratch, limit_mib, name, flops=0):
    return pl.pallas_call(
        kernel,
        out_shape=[jax.ShapeDtypeStruct(s, d) for s, d in outs],
        in_specs=specs,
        out_specs=[VMEM] * len(outs),
        scratch_shapes=scratch,
        compiler_params=pltpu.CompilerParams(vmem_limit_bytes=limit_mib << 20),
        name=name,
    )


def weights_kernel(w_a, w_b, w_c, gain, weights, half, gain_here, sems):
    copies = [pltpu.make_async_copy(gain, gain_here, sems.at[3])]
    for which, ref in enumerate((w_a, w_b, w_c)):
        copies.append(pltpu.make_async_copy(ref.at[0], weights.at[rows(which, H)], sems.at[which]))
    for copy in copies:
        copy.start()
    copies[0].wait()
    rest = jnp.broadcast_to(gain_here[0:1, :], (16, H))
    high = rest.astype(BF16).astype(F32)
    rest = rest - high
    mid = rest.astype(BF16).astype(F32)
    low = rest - mid
    row = lax.broadcasted_iota(jnp.int32, (16, H), 0)
    terms = jnp.where(row == 0, high, jnp.where(row == 1, mid, jnp.where(row == 2, low, 0.0)))
    weights[3 * H : 3 * H + 16, :] = terms.astype(BF16)
    weights[3 * H + 16 : 3 * H + 32, :] = jnp.zeros((16, H), BF16)
    for copy in copies[1:]:
        copy.wait()
    core = lax.axis_index("core")
    half[...] = weights[pl.ds(pl.multiple_of(core * W_HALF, 16), W_HALF), :]


def prepare_kernel(source, live, latent, cotangent, tiles, own, value, slope, tile, index, count, sems):
    sample = lax.axis_index("section")
    copies = [
        pltpu.make_async_copy(tiles, tile, sems.at[0]),
        pltpu.make_async_copy(source, index, sems.at[1]),
        pltpu.make_async_copy(live, count, sems.at[2]),
        pltpu.make_async_copy(latent.at[sample], value, sems.at[3]),
        pltpu.make_async_copy(cotangent.at[sample], slope, sems.at[4]),
    ]
    for copy in copies:
        copy.start()
    for copy in copies[:3]:
        copy.wait()
    slots = tile.shape[0]
    base = 2 * (lax.axis_index("chip") - 1)
    for column in range(6):
        total = jnp.zeros((B, B), F32)
        for slot in range(slots):
            hit = (index[slot] - base == column) & (slot < count[0])
            total = total + jnp.where(hit, tile[slot].astype(F32), 0.0)
        own[:, H + column * B : H + (column + 1) * B] = total.astype(BF16)
    for copy in copies[3:]:
        copy.wait()
    own[:, 0:H] = value[...]
    own[:, H + BAND :] = slope[...]


def pack_kernel(own, partner, pair, near, value):
    core = lax.axis_index("core")
    for ref, held in ((own, core), (partner, 1 - core)):
        pair[rows(held, B), :] = ref[...]
        near[rows(held, B), :] = ref[:, 0 : H + BAND]
        value[rows(held, B), :] = ref[:, 0:H]


def layer_gain(weights, layer):
    terms = weights[layer * W_ROWS + 3 * H : layer * W_ROWS + 3 * H + 16, :].astype(F32)
    return jnp.sum(terms, axis=0, keepdims=True)


def weight(weights, layer, which):
    start = layer * W_ROWS + which * H
    return weights[start : start + H, :]


def forward_kernel(
    own, m1, m2, m3, m4, t1, t2, t3, t4, w_own, w_m, w_t, w_mh, w_th,
    latents, grad_pre, turned, v3_out, v2_out, v1_out, f2_out, f1_out, f0_out, weights, w_low,
    v_a, v_b, band, unit, source,
):
    section, core = lax.axis_index("section"), lax.axis_index("core")
    weights[pl.ds(pl.multiple_of(section * W_ROWS, 16), W_ROWS), :] = w_own[...]
    before, after = (section + 3) % 4, (section + 1) % 4
    mine = jnp.where(core == 0, before, after)
    theirs = jnp.where(core == 0, after, before)
    far = (section + 2) % 4
    weights[pl.ds(pl.multiple_of(mine * W_ROWS, 16), W_ROWS), :] = w_m[...]
    weights[pl.ds(pl.multiple_of(theirs * W_ROWS, 16), W_ROWS), :] = w_t[...]
    weights[pl.ds(pl.multiple_of(far * W_ROWS + core * W_HALF, 16), W_HALF), :] = w_mh[...]
    weights[pl.ds(pl.multiple_of(far * W_ROWS + (1 - core) * W_HALF, 16), W_HALF), :] = w_th[...]

    v_a[rows(REACH), :] = own[:, 0:H]
    band[rows(REACH - 1), :] = own[:, H : H + BAND]
    for step, (m, t) in enumerate(((m1, t1), (m2, t2), (m3, t3), (m4, t4)), start=1):
        at_m = REACH - step + 2 * step * core
        at_t = 2 * REACH - at_m
        v_a[rows(at_m), :] = m[:, 0:H]
        v_a[rows(at_t), :] = t[:, 0:H]
        if step < REACH:
            band[rows(at_m - 1), :] = m[:, H : H + BAND]
            band[rows(at_t - 1), :] = t[:, H : H + BAND]

    w_low[...] = weights[0 : 2 * W_ROWS, :]
    now, later = v_a, v_b
    for layer in range(4):
        low, high = layer, 2 * REACH - layer
        gain = layer_gain(weights, layer)

        def project(j):
            value, _ = normed_rows(now[rows(j), :])
            held = (value * gain).astype(BF16)
            unit[rows(j), :] = held
            source[rows(j), :] = dot(held, weight(weights, layer, 0)).astype(BF16)

        def update(j):
            pre = dot(band[rows(j - 1), :], source[(j - 1) * PAIR : (j - 1) * PAIR + BAND, :])
            pre = pre + dot(unit[rows(j), :], weight(weights, layer, 1))
            sigma = 0.5 + 0.5 * jnp.tanh(0.5 * pre)
            act = (pre * sigma).astype(BF16)
            value = now[rows(j), :].astype(F32) + dot(act, weight(weights, layer, 2))
            later[rows(j), :] = value.astype(BF16)
            reach = (1, 2, 1, 0)[layer]
            if abs(j - REACH) <= reach:
                factor = sigma * (1.0 + pre * (1.0 - sigma))
                if layer == 3:
                    incoming = dot_t(own[:, H + BAND :], weight(weights, 3, 2))
                    grad_pre[...] = (incoming * factor).astype(BF16)
                else:
                    out = (f0_out, f1_out, f2_out)[layer]
                    out[rows(j - REACH + reach), :] = factor.astype(BF16)

        for j in range(low, low + 3):
            project(j)
        for j in range(low + 1, high):
            update(j)
            if j + 2 <= high:
                project(j + 2)
        latents[layer] = later[pl.ds(pl.multiple_of(REACH * PAIR + core * B, B), B), :]
        if layer == 0:
            v1_out[...] = later[3 * PAIR : 6 * PAIR, :]
        if layer == 1:
            v2_out[...] = later[4 * PAIR : 5 * PAIR, :]
        if layer == 2:
            v3_out[...] = later[3 * PAIR : 6 * PAIR, :]
        now, later = later, now

    for j in range(3, 6):
        for i in range(j - 1, j + 2):
            column = (j - i + 1) * PAIR
            piece = band[(i - 1) * PAIR : i * PAIR, column : column + PAIR]
            turned[(j - 3) * PAIR : (j - 2) * PAIR, (i - j + 1) * PAIR : (i - j + 2) * PAIR] = (
                piece.astype(F32).T.astype(BF16)
            )


def grad_pair(gradient, grad_pre, window, turned, values, weights, layer):
    back = dot(turned, window).astype(BF16)
    grad_unit = dot_t(grad_pre, weight(weights, layer, 1))
    grad_unit = grad_unit + dot_t(back, weight(weights, layer, 0))
    normed, inv = normed_rows(values)
    e = grad_unit * layer_gain(weights, layer)
    grad_in = inv * (
        e
        - jnp.mean(e, axis=-1, keepdims=True)
        - normed * jnp.mean(e * normed, axis=-1, keepdims=True)
    )
    return (gradient.astype(F32) + grad_in).astype(BF16)


def place(target, own, sides, core):
    middle = len(sides)
    target[rows(middle), :] = own[...]
    for step, (mine, theirs) in enumerate(sides, start=1):
        at_m = middle - step + 2 * step * core
        target[rows(at_m), :] = mine[...]
        target[rows(2 * middle - at_m), :] = theirs[...]


def backward_a_kernel(
    grad_pre, r1, r2, o1, o2, own, m1, t1, turned, v3, v2, f2, weights,
    g3_out, g2_out, held, cot, g3, gp2,
):
    core = lax.axis_index("core")
    place(held, grad_pre, ((r1, o1), (r2, o2)), core)
    cot[rows(1), :] = own[:, H + BAND :]
    cot[rows(2 * core), :] = m1[:, H + BAND :]
    cot[rows(2 - 2 * core), :] = t1[:, H + BAND :]
    for j in range(3):
        g3[rows(j), :] = grad_pair(
            cot[rows(j), :], held[rows(j + 1), :], held[j * PAIR : j * PAIR + BAND, :],
            turned[rows(j), :], v3[rows(j), :], weights, 3,
        )
        gp2[rows(j), :] = (dot_t(g3[rows(j), :], weight(weights, 2, 2)) * f2[rows(j), :]).astype(BF16)
    g3_out[...] = g3[pl.ds(pl.multiple_of(PAIR + core * B, B), B), :]
    g2_out[...] = grad_pair(
        g3[rows(1), :], gp2[rows(1), :], gp2[...], turned[rows(1), :], v2[...], weights, 2
    )


def backward_b_kernel(
    g2_own, r1, r2, o1, o2, g3_mine, turned, v1, own, f1, f0, weights,
    grads, g2, gp1, g1, gp0,
):
    core = lax.axis_index("core")
    place(g2, g2_own, ((r1, o1), (r2, o2)), core)
    for j in range(5):
        gp1[rows(j), :] = (dot_t(g2[rows(j), :], weight(weights, 1, 2)) * f1[rows(j), :]).astype(BF16)
    for j in range(3):
        g1[rows(j), :] = grad_pair(
            g2[rows(j + 1), :], gp1[rows(j + 1), :], gp1[j * PAIR : j * PAIR + BAND, :],
            turned[rows(j), :], v1[rows(j), :], weights, 1,
        )
        gp0[rows(j), :] = (dot_t(g1[rows(j), :], weight(weights, 0, 2)) * f0[rows(j), :]).astype(BF16)
    mine = pl.ds(pl.multiple_of(PAIR + core * B, B), B)
    grads[3] = g3_mine[...]
    grads[2] = g2_own[rows(core, B), :]
    grads[1] = g1[mine, :]
    g0 = grad_pair(g1[rows(1), :], gp0[rows(1), :], gp0[...], turned[rows(1), :], own[:, 0:H], weights, 0)
    g1[rows(1), :] = g0
    grads[0] = g1[mine, :]


def swap(value):
    return lax.ppermute(value, "core", [(0, 1), (1, 0)])


def spread(value, steps):
    chips = lax.axis_size("chip")
    pairs = []
    for c in range(chips):
        if c + steps < chips:
            pairs.append((2 * c, 2 * (c + steps)))
        if c - steps >= 0:
            pairs.append((2 * c + 1, 2 * (c - steps) + 1))
    return lax.ppermute(value, ("chip", "core"), pairs)


def around(value):
    count = lax.axis_size("section")
    pairs = []
    for s in range(count):
        pairs.append((2 * s, 2 * ((s + 1) % count)))
        pairs.append((2 * s + 1, 2 * ((s - 1) % count) + 1))
    return lax.ppermute(value, ("section", "core"), pairs)


def opposite(value):
    count = lax.axis_size("section")
    return lax.ppermute(value, "section", [(s, (s + count // 2) % count) for s in range(count)])


def to_layers(stacked, section):
    count = stacked.shape[0]
    out = jnp.zeros_like(stacked)
    keep = lax.dynamic_index_in_dim(stacked, section, 0, keepdims=True)
    out = lax.dynamic_update_slice_in_dim(out, keep, section, 0)
    for step in range(1, count):
        piece = lax.dynamic_index_in_dim(stacked, (section + step) % count, 0, keepdims=True)
        got = lax.ppermute(piece, "section", [(s, (s + step) % count) for s in range(count)])
        out = lax.dynamic_update_slice_in_dim(out, got, (section - step) % count, 0)
    return out


def body(latent, cotangent, w_a, w_b, w_c, gain, tiles, pair_source, live_pairs):
    section = lax.axis_index("section")
    wide = H + BAND

    w_own, w_half = call(
        weights_kernel,
        [((W_ROWS, H), BF16), ((W_HALF, H), BF16)],
        [HBM] * 4,
        [pltpu.VMEM((1, H), F32), pltpu.SemaphoreType.DMA((4,))],
        4,
        "weights",
    )(w_a, w_b, w_c, gain)
    w_m, w_mh = around(w_own), opposite(w_half)
    (own,) = call(
        prepare_kernel,
        [((B, wide + H), BF16)],
        [HBM] * 5,
        [
            pltpu.VMEM((B, H), BF16), pltpu.VMEM((B, H), BF16), pltpu.VMEM(tiles.shape, BF16),
            pltpu.SMEM(pair_source.shape, jnp.int32), pltpu.SMEM(live_pairs.shape, jnp.int32),
            pltpu.SemaphoreType.DMA((5,)),
        ],
        4,
        "prepare",
    )(pair_source, live_pairs, latent, cotangent, tiles)
    pair, near, value = call(
        pack_kernel,
        [((PAIR, wide + H), BF16), ((PAIR, wide), BF16), ((PAIR, H), BF16)],
        [VMEM] * 2,
        [],
        4,
        "pack",
    )(own, swap(own))
    m1, m2, m3, m4 = spread(pair, 1), spread(near, 2), spread(near, 3), spread(value, 4)
    w_m, m1, m2, m3, m4 = lax.optimization_barrier((w_m, m1, m2, m3, m4))
    w_t, w_th = swap(w_m), swap(w_mh)
    t1, t2, t3, t4 = swap(m1), swap(m2), swap(m3), swap(m4)

    span = 2 * REACH + 1
    latents, grad_pre, turned, v3, v2, v1, f2, f1, f0, weights, w_low = call(
        forward_kernel,
        [
            ((4, B, H), BF16), ((PAIR, H), BF16), ((3 * PAIR, BAND), BF16),
            ((3 * PAIR, H), BF16), ((PAIR, H), BF16), ((3 * PAIR, H), BF16),
            ((3 * PAIR, H), BF16), ((5 * PAIR, H), BF16), ((3 * PAIR, H), BF16),
            ((4 * W_ROWS, H), BF16), ((2 * W_ROWS, H), BF16),
        ],
        [VMEM] * 14,
        [
            pltpu.VMEM((span * PAIR, H), BF16), pltpu.VMEM((span * PAIR, H), BF16),
            pltpu.VMEM(((span - 2) * PAIR, BAND), BF16),
            pltpu.VMEM((span * PAIR, H), BF16), pltpu.VMEM((span * PAIR, H), BF16),
        ],
        FWD_MIB,
        "forward",
    )(pair, m1, m2, m3, m4, t1, t2, t3, t4, w_own, w_m, w_t, w_mh, w_th)

    r1, r2 = spread(grad_pre, 1), spread(grad_pre, 2)
    g3, g2 = call(
        backward_a_kernel,
        [((B, H), BF16), ((PAIR, H), BF16)],
        [VMEM] * 13,
        [
            pltpu.VMEM((5 * PAIR, H), BF16), pltpu.VMEM((3 * PAIR, H), BF16),
            pltpu.VMEM((3 * PAIR, H), BF16), pltpu.VMEM((3 * PAIR, H), BF16),
        ],
        BWD_MIB,
        "backward_a",
    )(grad_pre, r1, r2, swap(r1), swap(r2), pair, m1, t1, turned, v3, v2, f2, weights)

    latent_result = to_layers(latents, section)

    r1, r2 = spread(g2, 1), spread(g2, 2)
    (grads,) = call(
        backward_b_kernel,
        [((4, B, H), BF16)],
        [VMEM] * 12,
        [
            pltpu.VMEM((5 * PAIR, H), BF16), pltpu.VMEM((5 * PAIR, H), BF16),
            pltpu.VMEM((3 * PAIR, H), BF16), pltpu.VMEM((3 * PAIR, H), BF16),
        ],
        BWD_MIB,
        "backward_b",
    )(g2, r1, r2, swap(r1), swap(r2), g3, turned, v1, pair, f1, f0, w_low)

    grad_result = to_layers(grads, section)
    return (latent_result[None], grad_result[None])


def solution(mesh):
    devices = np.asarray(mesh.devices)
    sections, parts = devices.shape
    split = Mesh(devices.reshape(sections, parts // 2, 2), ("section", "chip", "core"))
    dom = ("chip", "core")
    in_specs = (
        P(None, dom, None),
        P(None, dom, None),
        P("section", None, None),
        P("section", None, None),
        P("section", None, None),
        P("section", None),
        P(dom, None, None),
        P(dom),
        P(dom),
    )
    out_specs = (P("section", None, dom, None), P("section", None, dom, None))
    return jax.shard_map(body, mesh=split, in_specs=in_specs, out_specs=out_specs, check_vma=False)
```

```python
import functools

import jax
import jax.numpy as jnp
import numpy as np
from jax import lax
from jax.experimental import pallas as pl
from jax.experimental.pallas import tpu as pltpu
from jax.sharding import Mesh, PartitionSpec as P

EPS = 1e-05
H = 512
B = 128
PAIR = 2 * B
BAND = 3 * PAIR
SENT = 5 * B
WIDE = H + SENT
REACH = 4
W_ROWS = 3 * H + 32
W_HALF = W_ROWS // 2
F32, BF16 = jnp.float32, jnp.bfloat16
VMEM = pl.BlockSpec(memory_space=pltpu.VMEM)
HBM = pl.BlockSpec(memory_space=pltpu.HBM)
ANY = pl.BlockSpec(memory_space=pl.ANY)
FWD_MIB, BWD_MIB = 24, 12


def rows(index, size=PAIR):
    if isinstance(index, int):
        return pl.ds(index * size, size)
    return pl.ds(pl.multiple_of(index * size, size), size)


def dot(a, b):
    return jnp.dot(a, b, preferred_element_type=F32)


def dot_t(a, b):
    return lax.dot_general(a, b, (((1,), (1,)), ((), ())), preferred_element_type=F32)


def normed_rows(values):
    wide = values.astype(F32)
    centre = wide - jnp.mean(wide, axis=-1, keepdims=True)
    inv = lax.rsqrt(jnp.mean(centre * centre, axis=-1, keepdims=True) + EPS)
    return centre * inv, inv


def call(kernel, outs, specs, scratch, limit_mib, name, out_specs=None, aliases=None, units=0):
    return pl.pallas_call(
        kernel,
        out_shape=[jax.ShapeDtypeStruct(s, d) for s, d in outs],
        in_specs=specs,
        out_specs=out_specs or [VMEM] * len(outs),
        input_output_aliases=aliases or {},
        cost_estimate=pl.CostEstimate(
            flops=units * 2 * B * H * H, bytes_accessed=units * 2 * B * H, transcendentals=0
        ),
        scratch_shapes=scratch,
        compiler_params=pltpu.CompilerParams(vmem_limit_bytes=limit_mib << 20),
        name=name,
    )


def weights_kernel(w_a, w_b, w_c, gain, weights, gain_here, terms, sems):
    copies = [
        pltpu.make_async_copy(ref.at[0], weights.at[rows(which, H)], sems.at[which])
        for which, ref in enumerate((w_a, w_b, w_c))
    ]
    first = pltpu.make_async_copy(gain, gain_here, sems.at[3])
    first.start()
    for copy in copies:
        copy.start()
    first.wait()
    rest = jnp.broadcast_to(gain_here[0:1, :], (32, H))
    high = rest.astype(BF16).astype(F32)
    rest = rest - high
    mid = rest.astype(BF16).astype(F32)
    low = rest - mid
    row = lax.broadcasted_iota(jnp.int32, (32, H), 0)
    held = jnp.where(row == 0, high, jnp.where(row == 1, mid, jnp.where(row == 2, low, 0.0)))
    terms[...] = held.astype(BF16)
    last = pltpu.make_async_copy(terms, weights.at[pl.ds(3 * H, 32)], sems.at[4])
    last.start()
    for copy in copies:
        copy.wait()
    last.wait()


def half_kernel(weights, half):
    core = lax.axis_index("core")
    half[...] = weights[pl.ds(pl.multiple_of(core * W_HALF, 16), W_HALF), :]


def prepare_kernel(source, live, latent, cotangent, tiles, own, value, slope, tile, index, count, sems):
    sample = lax.axis_index("section")
    copies = [
        pltpu.make_async_copy(tiles, tile, sems.at[0]),
        pltpu.make_async_copy(source, index, sems.at[1]),
        pltpu.make_async_copy(live, count, sems.at[2]),
        pltpu.make_async_copy(latent.at[sample], value, sems.at[3]),
        pltpu.make_async_copy(cotangent.at[sample], slope, sems.at[4]),
    ]
    for copy in copies:
        copy.start()
    for copy in copies[:3]:
        copy.wait()
    slots = tile.shape[0]
    base = 2 * lax.axis_index("chip") + lax.axis_index("core") - 2
    for column in range(5):
        total = jnp.zeros((B, B), F32)
        for slot in range(slots):
            hit = (index[slot] - base == column) & (slot < count[0])
            total = total + jnp.where(hit, tile[slot].astype(F32), 0.0)
        own[:, H + column * B : H + (column + 1) * B] = total.astype(BF16)
    for copy in copies[3:]:
        copy.wait()
    own[:, 0:H] = value[...]
    own[:, WIDE:] = slope[...]


def pack_kernel(own, partner, near, value, slope):
    core = lax.axis_index("core")
    for ref, held in ((own, core), (partner, 1 - core)):
        near[rows(held, B), :] = ref[:, 0:WIDE]
        value[rows(held, B), :] = ref[:, 0:H]
        slope[rows(held, B), :] = ref[:, WIDE:]


def layer_gain(weights, layer):
    terms = weights[layer * W_ROWS + 3 * H : layer * W_ROWS + 3 * H + 16, :].astype(F32)
    return jnp.sum(terms, axis=0, keepdims=True)


def weight(weights, layer, which):
    start = layer * W_ROWS + which * H
    return weights[start : start + H, :]


def send_pieces(stacked, pieces, section):
    for step, piece in enumerate(pieces):
        piece[...] = stacked[(section + step) % 4]


def forward_kernel(
    own, cotangent, m1, m2, m3, m4, t1, t2, t3, t4, w_own, w_m, w_t, w_mh, w_th, _,
    l0, l1, l2, l3, grad_pre, turned, v3_out, v2_out, v1_out, f2_out, f1_out, f0_out, weights,
    latents, v_a, v_b, band, unit, source,
):
    section, core = lax.axis_index("section"), lax.axis_index("core")
    weights[pl.ds(pl.multiple_of(section * W_ROWS, 16), W_ROWS), :] = w_own[...]
    before, after = (section + 3) % 4, (section + 1) % 4
    mine = jnp.where(core == 0, before, after)
    theirs = jnp.where(core == 0, after, before)
    far = (section + 2) % 4
    weights[pl.ds(pl.multiple_of(mine * W_ROWS, 16), W_ROWS), :] = w_m[...]
    weights[pl.ds(pl.multiple_of(theirs * W_ROWS, 16), W_ROWS), :] = w_t[...]
    weights[pl.ds(pl.multiple_of(far * W_ROWS + core * W_HALF, 16), W_HALF), :] = w_mh[...]
    weights[pl.ds(pl.multiple_of(far * W_ROWS + (1 - core) * W_HALF, 16), W_HALF), :] = w_th[...]

    def put_band(at, ref):
        for k in range(2):
            row = pl.ds(pl.multiple_of(at * PAIR + k * B, B), B)
            band[row, k * B : k * B + SENT] = ref[k * B : (k + 1) * B, H:WIDE]
            rim = (1 - k) * SENT
            band[row, rim : rim + B] = jnp.zeros((B, B), BF16)

    v_a[rows(REACH), :] = own[:, 0:H]
    put_band(REACH - 1, own)
    for step, (m, t) in enumerate(((m1, t1), (m2, t2), (m3, t3), (m4, t4)), start=1):
        at_m = REACH - step + 2 * step * core
        at_t = 2 * REACH - at_m
        v_a[rows(at_m), :] = m[:, 0:H]
        v_a[rows(at_t), :] = t[:, 0:H]
        if step < REACH:
            put_band(at_m - 1, m)
            put_band(at_t - 1, t)

    now, later = v_a, v_b
    for layer in range(4):
        low, high = layer, 2 * REACH - layer
        gain = layer_gain(weights, layer)

        def project(j):
            value, _ = normed_rows(now[rows(j), :])
            held = (value * gain).astype(BF16)
            unit[rows(j), :] = held
            source[rows(j), :] = dot(held, weight(weights, layer, 0)).astype(BF16)

        def update(j):
            pre = dot(band[rows(j - 1), :], source[(j - 1) * PAIR : (j - 1) * PAIR + BAND, :])
            pre = pre + dot(unit[rows(j), :], weight(weights, layer, 1))
            sigma = 0.5 + 0.5 * jnp.tanh(0.5 * pre)
            act = (pre * sigma).astype(BF16)
            value = now[rows(j), :].astype(F32) + dot(act, weight(weights, layer, 2))
            later[rows(j), :] = value.astype(BF16)
            reach = (1, 2, 1, 0)[layer]
            if abs(j - REACH) <= reach:
                factor = sigma * (1.0 + pre * (1.0 - sigma))
                if layer == 3:
                    incoming = dot_t(cotangent[...], weight(weights, 3, 2))
                    grad_pre[...] = (incoming * factor).astype(BF16)
                else:
                    out = (f0_out, f1_out, f2_out)[layer]
                    out[rows(j - REACH + reach), :] = factor.astype(BF16)

        for j in range(low, low + 3):
            project(j)
        for j in range(low + 1, high):
            update(j)
            if j + 2 <= high:
                project(j + 2)
        latents[layer] = later[pl.ds(pl.multiple_of(REACH * PAIR + core * B, B), B), :]
        if layer == 0:
            v1_out[...] = later[3 * PAIR : 6 * PAIR, :]
        if layer == 1:
            v2_out[...] = later[4 * PAIR : 5 * PAIR, :]
        if layer == 2:
            v3_out[...] = later[3 * PAIR : 6 * PAIR, :]
        now, later = later, now
    send_pieces(latents, (l0, l1, l2, l3), section)

    for j in range(3, 6):
        for i in range(j - 1, j + 2):
            column = (j - i + 1) * PAIR
            piece = band[(i - 1) * PAIR : i * PAIR, column : column + PAIR]
            turned[(j - 3) * PAIR : (j - 2) * PAIR, (i - j + 1) * PAIR : (i - j + 2) * PAIR] = (
                piece.astype(F32).T.astype(BF16)
            )


def grad_pair(gradient, grad_pre, window, turned, values, weights, layer):
    back = dot(turned, window).astype(BF16)
    grad_unit = dot_t(grad_pre, weight(weights, layer, 1))
    grad_unit = grad_unit + dot_t(back, weight(weights, layer, 0))
    normed, inv = normed_rows(values)
    e = grad_unit * layer_gain(weights, layer)
    grad_in = inv * (
        e
        - jnp.mean(e, axis=-1, keepdims=True)
        - normed * jnp.mean(e * normed, axis=-1, keepdims=True)
    )
    return (gradient.astype(F32) + grad_in).astype(BF16)


def place(target, own, sides, core):
    middle = len(sides)
    target[rows(middle), :] = own[...]
    for step, (mine, theirs) in enumerate(sides, start=1):
        at_m = middle - step + 2 * step * core
        target[rows(at_m), :] = mine[...]
        target[rows(2 * middle - at_m), :] = theirs[...]


def backward_a_kernel(
    grad_pre, r1, r2, o1, o2, own, c1, d1, v3, v2, f2, turned, v1, f1, f0, weights,
    g3_out, g2_out, kept_turned, kept_v1, kept_f1, kept_f0, kept_weights, held, cot, g3, gp2,
):
    core = lax.axis_index("core")
    place(held, grad_pre, ((r1, o1), (r2, o2)), core)
    place(cot, own, ((c1, d1),), core)
    for j in range(3):
        g3[rows(j), :] = grad_pair(
            cot[rows(j), :], held[rows(j + 1), :], held[j * PAIR : j * PAIR + BAND, :],
            turned[rows(j), :], v3[rows(j), :], weights, 3,
        )
        gp2[rows(j), :] = (dot_t(g3[rows(j), :], weight(weights, 2, 2)) * f2[rows(j), :]).astype(BF16)
    g3_out[...] = g3[pl.ds(pl.multiple_of(PAIR + core * B, B), B), :]
    g2_out[...] = grad_pair(
        g3[rows(1), :], gp2[rows(1), :], gp2[...], turned[rows(1), :], v2[...], weights, 2
    )


def backward_b_kernel(
    g2_own, r1, r2, o1, o2, g3_mine, turned, v1, own, f1, f0, weights,
    p0, p1, p2, p3, grads, g2, gp1, g1, gp0,
):
    core = lax.axis_index("core")
    place(g2, g2_own, ((r1, o1), (r2, o2)), core)
    for j in range(5):
        gp1[rows(j), :] = (dot_t(g2[rows(j), :], weight(weights, 1, 2)) * f1[rows(j), :]).astype(BF16)
    for j in range(3):
        g1[rows(j), :] = grad_pair(
            g2[rows(j + 1), :], gp1[rows(j + 1), :], gp1[j * PAIR : j * PAIR + BAND, :],
            turned[rows(j), :], v1[rows(j), :], weights, 1,
        )
        gp0[rows(j), :] = (dot_t(g1[rows(j), :], weight(weights, 0, 2)) * f0[rows(j), :]).astype(BF16)
    mine = pl.ds(pl.multiple_of(PAIR + core * B, B), B)
    grads[3] = g3_mine[...]
    grads[2] = g2_own[rows(core, B), :]
    grads[1] = g1[mine, :]
    g0 = grad_pair(g1[rows(1), :], gp0[rows(1), :], gp0[...], turned[rows(1), :], own[...], weights, 0)
    g1[rows(1), :] = g0
    grads[0] = g1[mine, :]
    send_pieces(grads, (p0, p1, p2, p3), lax.axis_index("section"))


def collect_kernel(l0, l1, l2, l3, g0, g1, g2, g3, latents, grads, sems):
    section = lax.axis_index("section")
    copies = []
    for side, (out, pieces) in enumerate(((latents, (l0, l1, l2, l3)), (grads, (g0, g1, g2, g3)))):
        for step, piece in enumerate(pieces):
            at = (section + 4 - step) % 4
            copies.append(pltpu.make_async_copy(piece, out.at[at], sems.at[4 * side + step]))
    for copy in copies:
        copy.start()
    for copy in copies:
        copy.wait()


def swap(value):
    return lax.ppermute(value, "core", [(0, 1), (1, 0)])


def spread(value, steps):
    chips = lax.axis_size("chip")
    pairs = []
    for c in range(chips):
        if c + steps < chips:
            pairs.append((2 * c, 2 * (c + steps)))
        if c - steps >= 0:
            pairs.append((2 * c + 1, 2 * (c - steps) + 1))
    return lax.ppermute(value, ("chip", "core"), pairs)


def around(value):
    count = lax.axis_size("section")
    pairs = []
    for s in range(count):
        pairs.append((2 * s, 2 * ((s + 1) % count)))
        pairs.append((2 * s + 1, 2 * ((s - 1) % count) + 1))
    return lax.ppermute(value, ("section", "core"), pairs)


def onward(value, steps):
    count = lax.axis_size("section")
    return lax.ppermute(value, "section", [(s, (s + steps) % count) for s in range(count)])


def body(latent, cotangent, w_a, w_b, w_c, gain, tiles, pair_source, live_pairs):
    section = lax.axis_index("section")

    (w_own,) = call(
        weights_kernel,
        [((W_ROWS, H), BF16)],
        [HBM] * 4,
        [pltpu.VMEM((1, H), F32), pltpu.VMEM((32, H), BF16), pltpu.SemaphoreType.DMA((5,))],
        56,
        "weights",
        out_specs=[HBM],
    )(w_a, w_b, w_c, gain)
    w_m = around(w_own)
    (own,) = call(
        prepare_kernel,
        [((B, WIDE + H), BF16)],
        [HBM] * 5,
        [
            pltpu.VMEM((B, H), BF16), pltpu.VMEM((B, H), BF16), pltpu.VMEM(tiles.shape, BF16),
            pltpu.SMEM(pair_source.shape, jnp.int32), pltpu.SMEM(live_pairs.shape, jnp.int32),
            pltpu.SemaphoreType.DMA((5,)),
        ],
        4,
        "prepare",
    )(pair_source, live_pairs, latent, cotangent, tiles)
    near, value, slope = call(
        pack_kernel,
        [((PAIR, WIDE), BF16), ((PAIR, H), BF16), ((PAIR, H), BF16)],
        [VMEM] * 2,
        [],
        4,
        "pack",
    )(own, swap(own))
    m1, m3, m4 = spread(near, 1), spread(near, 3), spread(value, 4)
    arrived, m4 = lax.optimization_barrier((w_m, m4))
    (w_half,) = call(half_kernel, [((W_HALF, H), BF16)], [VMEM], [], 4, "half")(arrived)
    w_mh = around(w_half)
    m2 = spread(m1, 1)
    w_m, m1, m3, m4, after = lax.optimization_barrier((w_m, m1, m3, m4, slope))
    c1 = spread(after, 1)
    d1 = swap(c1)
    w_t, w_th = swap(w_m), swap(w_mh)
    t1, t2, t3, t4 = swap(m1), swap(m2), swap(m3), swap(m4)

    span = 2 * REACH + 1
    l0, l1, l2, l3, grad_pre, turned, v3, v2, v1, f2, f1, f0, weights = call(
        forward_kernel,
        [
            ((B, H), BF16), ((B, H), BF16), ((B, H), BF16), ((B, H), BF16),
            ((PAIR, H), BF16), ((3 * PAIR, BAND), BF16),
            ((3 * PAIR, H), BF16), ((PAIR, H), BF16), ((3 * PAIR, H), BF16),
            ((3 * PAIR, H), BF16), ((5 * PAIR, H), BF16), ((3 * PAIR, H), BF16),
            ((4 * W_ROWS, H), BF16),
        ],
        [VMEM] * 15 + [ANY],
        [
            pltpu.VMEM((4, B, H), BF16),
            pltpu.VMEM((span * PAIR, H), BF16), pltpu.VMEM((span * PAIR, H), BF16),
            pltpu.VMEM(((span - 2) * PAIR, BAND), BF16),
            pltpu.VMEM((span * PAIR, H), BF16), pltpu.VMEM((span * PAIR, H), BF16),
        ],
        FWD_MIB,
        "forward",
        units=160,
    )(near, slope, m1, m2, m3, m4, t1, t2, t3, t4, w_own, w_m, w_t, w_mh, w_th, d1)

    latents = [onward(l1, 1), onward(l2, 2), onward(l3, 3)]
    r1 = spread(grad_pre, 1)
    r2 = spread(r1, 1)
    kept = [turned, v1, f1, f0, weights]
    g3, g2, turned, v1, f1, f0, weights = call(
        backward_a_kernel,
        [((B, H), BF16), ((PAIR, H), BF16)] + [(k.shape, k.dtype) for k in kept],
        [VMEM] * 12 + [ANY] * 3 + [VMEM],
        [
            pltpu.VMEM((5 * PAIR, H), BF16), pltpu.VMEM((3 * PAIR, H), BF16),
            pltpu.VMEM((3 * PAIR, H), BF16), pltpu.VMEM((3 * PAIR, H), BF16),
        ],
        BWD_MIB,
        "backward_a",
        out_specs=[VMEM] * 2 + [ANY] * len(kept),
        aliases={11 + i: 2 + i for i in range(len(kept))},
        units=60,
    )(grad_pre, r1, r2, swap(r1), swap(r2), slope, c1, d1, v3, v2, f2, *kept)

    r1 = spread(g2, 1)
    r2 = spread(r1, 1)
    grads = call(
        backward_b_kernel,
        [((B, H), BF16)] * 4,
        [VMEM] * 12,
        [
            pltpu.VMEM((4, B, H), BF16),
            pltpu.VMEM((5 * PAIR, H), BF16), pltpu.VMEM((5 * PAIR, H), BF16),
            pltpu.VMEM((3 * PAIR, H), BF16), pltpu.VMEM((3 * PAIR, H), BF16),
        ],
        BWD_MIB,
        "backward_b",
        units=70,
    )(g2, r1, r2, swap(r1), swap(r2), g3, turned, v1, value, f1, f0, weights)

    moved = [onward(piece, step) for step, piece in enumerate(grads) if step]
    latent_result, grad_result = call(
        collect_kernel,
        [((4, B, H), BF16)] * 2,
        [VMEM] * 8,
        [pltpu.SemaphoreType.DMA((8,))],
        4,
        "collect",
        out_specs=[HBM] * 2,
    )(l0, *latents, grads[0], *moved)
    return (latent_result[None], grad_result[None])


def solution(mesh):
    devices = np.asarray(mesh.devices)
    sections, parts = devices.shape
    split = Mesh(devices.reshape(sections, parts // 2, 2), ("section", "chip", "core"))
    dom = ("chip", "core")
    in_specs = (
        P(None, dom, None),
        P(None, dom, None),
        P("section", None, None),
        P("section", None, None),
        P("section", None, None),
        P("section", None),
        P(dom, None, None),
        P(dom),
        P(dom),
    )
    out_specs = (P("section", None, dom, None), P("section", None, dom, None))
    return jax.shard_map(body, mesh=split, in_specs=in_specs, out_specs=out_specs, check_vma=False)
```

```python
import functools

import jax
import jax.numpy as jnp
import numpy as np
from jax import lax
from jax.experimental import pallas as pl
from jax.experimental.pallas import tpu as pltpu
from jax.sharding import Mesh, PartitionSpec as P

EPS = 1e-05
H = 512
B = 128
PAIR = 2 * B
BAND = 3 * PAIR
SENT = 5 * B
WIDE = H + SENT
AT3 = WIDE + H
AT4 = AT3 + WIDE
REACH = 4
W_ROWS = 3 * H + 32
W_HALF = W_ROWS // 2
F32, BF16 = jnp.float32, jnp.bfloat16
VMEM = pl.BlockSpec(memory_space=pltpu.VMEM)
HBM = pl.BlockSpec(memory_space=pltpu.HBM)
ANY = pl.BlockSpec(memory_space=pl.ANY)
FWD_MIB, BWD_MIB, WGT_MIB = 24, 12, 58


def rows(index, size=PAIR):
    if isinstance(index, int):
        return pl.ds(index * size, size)
    return pl.ds(pl.multiple_of(index * size, size), size)


def dot(a, b):
    return jnp.dot(a, b, preferred_element_type=F32)


def dot_t(a, b):
    return lax.dot_general(a, b, (((1,), (1,)), ((), ())), preferred_element_type=F32)


def normed_rows(values):
    wide = values.astype(F32)
    centre = wide - jnp.mean(wide, axis=-1, keepdims=True)
    inv = lax.rsqrt(jnp.mean(centre * centre, axis=-1, keepdims=True) + EPS)
    return centre * inv, inv


def call(kernel, outs, specs, scratch, limit_mib, name, out_specs=None, aliases=None, units=0):
    return pl.pallas_call(
        kernel,
        out_shape=[jax.ShapeDtypeStruct(s, d) for s, d in outs],
        in_specs=specs,
        out_specs=out_specs or [VMEM] * len(outs),
        input_output_aliases=aliases or {},
        cost_estimate=pl.CostEstimate(
            flops=units * 2 * B * H * H, bytes_accessed=units * 2 * B * H, transcendentals=0
        ),
        scratch_shapes=scratch,
        compiler_params=pltpu.CompilerParams(vmem_limit_bytes=limit_mib << 20),
        name=name,
    )


def weights_kernel(w_a, w_b, w_c, gain, weights, gain_here, sems):
    copies = [
        pltpu.make_async_copy(ref.at[0], weights.at[rows(which, H)], sems.at[which])
        for which, ref in enumerate((w_a, w_b, w_c))
    ]
    first = pltpu.make_async_copy(gain, gain_here, sems.at[3])
    first.start()
    for copy in copies:
        copy.start()
    first.wait()
    rest = jnp.broadcast_to(gain_here[0:1, :], (32, H))
    high = rest.astype(BF16).astype(F32)
    rest = rest - high
    mid = rest.astype(BF16).astype(F32)
    low = rest - mid
    row = lax.broadcasted_iota(jnp.int32, (32, H), 0)
    held = jnp.where(row == 0, high, jnp.where(row == 1, mid, jnp.where(row == 2, low, 0.0)))
    weights[3 * H : 3 * H + 32, :] = held.astype(BF16)
    for copy in copies:
        copy.wait()


def half_kernel(weights, half):
    core = lax.axis_index("core")
    half[...] = weights[pl.ds(pl.multiple_of(core * W_HALF, 16), W_HALF), :]


def prepare_kernel(source, live, latent, cotangent, tiles, own, value, slope, tile, index, count, sems):
    sample = lax.axis_index("section")
    copies = [
        pltpu.make_async_copy(tiles, tile, sems.at[0]),
        pltpu.make_async_copy(source, index, sems.at[1]),
        pltpu.make_async_copy(live, count, sems.at[2]),
        pltpu.make_async_copy(latent.at[sample], value, sems.at[3]),
        pltpu.make_async_copy(cotangent.at[sample], slope, sems.at[4]),
    ]
    for copy in copies:
        copy.start()
    for copy in copies[:3]:
        copy.wait()
    slots = tile.shape[0]
    base = 2 * lax.axis_index("chip") + lax.axis_index("core") - 2
    for column in range(5):
        total = jnp.zeros((B, B), F32)
        for slot in range(slots):
            hit = (index[slot] - base == column) & (slot < count[0])
            total = total + jnp.where(hit, tile[slot].astype(F32), 0.0)
        own[:, H + column * B : H + (column + 1) * B] = total.astype(BF16)
    for copy in copies[3:]:
        copy.wait()
    own[:, 0:H] = value[...]
    own[:, WIDE:] = slope[...]


def pack_kernel(own, partner, first, near, value):
    core = lax.axis_index("core")
    for ref, held in ((own, core), (partner, 1 - core)):
        first[rows(held, B), :] = ref[...]
        near[rows(held, B), :] = ref[:, 0:WIDE]
        value[rows(held, B), :] = ref[:, 0:H]


def join_kernel(m1, m3, m4, joined, near):
    joined[:, 0:AT3] = m1[...]
    joined[:, AT3:AT4] = m3[...]
    joined[:, AT4:] = m4[...]
    near[...] = m1[:, 0:WIDE]


def layer_gain(weights, layer):
    terms = weights[layer * W_ROWS + 3 * H : layer * W_ROWS + 3 * H + 16, :].astype(F32)
    return jnp.sum(terms, axis=0, keepdims=True)


def weight(weights, layer, which):
    start = layer * W_ROWS + which * H
    return weights[start : start + H, :]


def send_pieces(stacked, pieces, section):
    for step, piece in enumerate(pieces):
        piece[...] = stacked[(section + step) % 4]


def forward_kernel(
    own, m1, m2, m3, m4, joined, t2, w_own, w_m, w_t, w_mh, w_th,
    l0, l1, l2, l3, grad_pre, turned, v3_out, v2_out, v1_out, f2_out, f1_out, f0_out, weights,
    latents, v_a, v_b, band, unit, source,
):
    section, core = lax.axis_index("section"), lax.axis_index("core")
    weights[pl.ds(pl.multiple_of(section * W_ROWS, 16), W_ROWS), :] = w_own[...]
    before, after = (section + 3) % 4, (section + 1) % 4
    mine = jnp.where(core == 0, before, after)
    theirs = jnp.where(core == 0, after, before)
    far = (section + 2) % 4
    weights[pl.ds(pl.multiple_of(mine * W_ROWS, 16), W_ROWS), :] = w_m[...]
    weights[pl.ds(pl.multiple_of(theirs * W_ROWS, 16), W_ROWS), :] = w_t[...]
    weights[pl.ds(pl.multiple_of(far * W_ROWS + core * W_HALF, 16), W_HALF), :] = w_mh[...]
    weights[pl.ds(pl.multiple_of(far * W_ROWS + (1 - core) * W_HALF, 16), W_HALF), :] = w_th[...]

    def put_band(at, ref):
        for k in range(2):
            row = pl.ds(pl.multiple_of(at * PAIR + k * B, B), B)
            band[row, k * B : k * B + SENT] = ref[k * B : (k + 1) * B, H:WIDE]
            rim = (1 - k) * SENT
            band[row, rim : rim + B] = jnp.zeros((B, B), BF16)

    t1, t3, t4 = joined.at[:, 0:AT3], joined.at[:, AT3:AT4], joined.at[:, AT4:]
    v_a[rows(REACH), :] = own[:, 0:H]
    put_band(REACH - 1, own)
    for step, (m, t) in enumerate(((m1, t1), (m2, t2), (m3, t3), (m4, t4)), start=1):
        at_m = REACH - step + 2 * step * core
        at_t = 2 * REACH - at_m
        v_a[rows(at_m), :] = m[:, 0:H]
        v_a[rows(at_t), :] = t[:, 0:H]
        if step < REACH:
            put_band(at_m - 1, m)
            put_band(at_t - 1, t)

    now, later = v_a, v_b
    for layer in range(4):
        low, high = layer, 2 * REACH - layer
        gain = layer_gain(weights, layer)

        def project(j):
            value, _ = normed_rows(now[rows(j), :])
            held = (value * gain).astype(BF16)
            unit[rows(j), :] = held
            source[rows(j), :] = dot(held, weight(weights, layer, 0)).astype(BF16)

        def update(j):
            pre = dot(band[rows(j - 1), :], source[(j - 1) * PAIR : (j - 1) * PAIR + BAND, :])
            pre = pre + dot(unit[rows(j), :], weight(weights, layer, 1))
            sigma = 0.5 + 0.5 * jnp.tanh(0.5 * pre)
            act = (pre * sigma).astype(BF16)
            value = now[rows(j), :].astype(F32) + dot(act, weight(weights, layer, 2))
            later[rows(j), :] = value.astype(BF16)
            reach = (1, 2, 1, 0)[layer]
            if abs(j - REACH) <= reach:
                factor = sigma * (1.0 + pre * (1.0 - sigma))
                if layer == 3:
                    incoming = dot_t(own[:, WIDE:], weight(weights, 3, 2))
                    grad_pre[...] = (incoming * factor).astype(BF16)
                else:
                    out = (f0_out, f1_out, f2_out)[layer]
                    out[rows(j - REACH + reach), :] = factor.astype(BF16)

        for j in range(low, low + 3):
            project(j)
        for j in range(low + 1, high):
            update(j)
            if j + 2 <= high:
                project(j + 2)
        latents[layer] = later[pl.ds(pl.multiple_of(REACH * PAIR + core * B, B), B), :]
        if layer == 0:
            v1_out[...] = later[3 * PAIR : 6 * PAIR, :]
        if layer == 1:
            v2_out[...] = later[4 * PAIR : 5 * PAIR, :]
        if layer == 2:
            v3_out[...] = later[3 * PAIR : 6 * PAIR, :]
        now, later = later, now
    send_pieces(latents, (l0, l1, l2, l3), section)

    for j in range(3, 6):
        for i in range(j - 1, j + 2):
            column = (j - i + 1) * PAIR
            piece = band[(i - 1) * PAIR : i * PAIR, column : column + PAIR]
            turned[(j - 3) * PAIR : (j - 2) * PAIR, (i - j + 1) * PAIR : (i - j + 2) * PAIR] = (
                piece.astype(F32).T.astype(BF16)
            )


def grad_pair(gradient, grad_pre, window, turned, values, weights, layer):
    back = dot(turned, window).astype(BF16)
    grad_unit = dot_t(grad_pre, weight(weights, layer, 1))
    grad_unit = grad_unit + dot_t(back, weight(weights, layer, 0))
    normed, inv = normed_rows(values)
    e = grad_unit * layer_gain(weights, layer)
    grad_in = inv * (
        e
        - jnp.mean(e, axis=-1, keepdims=True)
        - normed * jnp.mean(e * normed, axis=-1, keepdims=True)
    )
    return (gradient.astype(F32) + grad_in).astype(BF16)


def place(target, own, sides, core):
    middle = len(sides)
    target[rows(middle), :] = own[...]
    for step, (mine, theirs) in enumerate(sides, start=1):
        at_m = middle - step + 2 * step * core
        target[rows(at_m), :] = mine[...]
        target[rows(2 * middle - at_m), :] = theirs[...]


def backward_a_kernel(
    grad_pre, r1, r2, o1, o2, own, m1, t1, v3, v2, f2, turned, v1, f1, f0, weights,
    g3_out, g2_out, kept_turned, kept_v1, kept_f1, kept_f0, kept_weights, held, cot, g3, gp2,
):
    core = lax.axis_index("core")
    place(held, grad_pre, ((r1, o1), (r2, o2)), core)
    place(cot, own.at[:, WIDE:], ((m1.at[:, WIDE:], t1.at[:, WIDE:AT3]),), core)
    for j in range(3):
        g3[rows(j), :] = grad_pair(
            cot[rows(j), :], held[rows(j + 1), :], held[j * PAIR : j * PAIR + BAND, :],
            turned[rows(j), :], v3[rows(j), :], weights, 3,
        )
        gp2[rows(j), :] = (dot_t(g3[rows(j), :], weight(weights, 2, 2)) * f2[rows(j), :]).astype(BF16)
    g3_out[...] = g3[pl.ds(pl.multiple_of(PAIR + core * B, B), B), :]
    g2_out[...] = grad_pair(
        g3[rows(1), :], gp2[rows(1), :], gp2[...], turned[rows(1), :], v2[...], weights, 2
    )


def backward_b_kernel(
    g2_own, r1, r2, o1, o2, g3_mine, turned, v1, own, f1, f0, weights,
    p0, p1, p2, p3, grads, g2, gp1, g1, gp0,
):
    core = lax.axis_index("core")
    place(g2, g2_own, ((r1, o1), (r2, o2)), core)
    for j in range(5):
        gp1[rows(j), :] = (dot_t(g2[rows(j), :], weight(weights, 1, 2)) * f1[rows(j), :]).astype(BF16)
    for j in range(3):
        g1[rows(j), :] = grad_pair(
            g2[rows(j + 1), :], gp1[rows(j + 1), :], gp1[j * PAIR : j * PAIR + BAND, :],
            turned[rows(j), :], v1[rows(j), :], weights, 1,
        )
        gp0[rows(j), :] = (dot_t(g1[rows(j), :], weight(weights, 0, 2)) * f0[rows(j), :]).astype(BF16)
    mine = pl.ds(pl.multiple_of(PAIR + core * B, B), B)
    grads[3] = g3_mine[...]
    grads[2] = g2_own[rows(core, B), :]
    grads[1] = g1[mine, :]
    g0 = grad_pair(g1[rows(1), :], gp0[rows(1), :], gp0[...], turned[rows(1), :], own[:, 0:H], weights, 0)
    g1[rows(1), :] = g0
    grads[0] = g1[mine, :]
    send_pieces(grads, (p0, p1, p2, p3), lax.axis_index("section"))


def collect_kernel(l0, l1, l2, l3, g0, g1, g2, g3, latents, grads, sems):
    section = lax.axis_index("section")
    copies = []
    for side, (out, pieces) in enumerate(((latents, (l0, l1, l2, l3)), (grads, (g0, g1, g2, g3)))):
        for step, piece in enumerate(pieces):
            at = (section + 4 - step) % 4
            copies.append(pltpu.make_async_copy(piece, out.at[at], sems.at[4 * side + step]))
    for copy in copies:
        copy.start()
    for copy in copies:
        copy.wait()


def swap(value):
    return lax.ppermute(value, "core", [(0, 1), (1, 0)])


def spread(value, steps):
    chips = lax.axis_size("chip")
    pairs = []
    for c in range(chips):
        if c + steps < chips:
            pairs.append((2 * c, 2 * (c + steps)))
        if c - steps >= 0:
            pairs.append((2 * c + 1, 2 * (c - steps) + 1))
    return lax.ppermute(value, ("chip", "core"), pairs)


def around(value):
    count = lax.axis_size("section")
    pairs = []
    for s in range(count):
        pairs.append((2 * s, 2 * ((s + 1) % count)))
        pairs.append((2 * s + 1, 2 * ((s - 1) % count) + 1))
    return lax.ppermute(value, ("section", "core"), pairs)


def onward(value, steps):
    count = lax.axis_size("section")
    return lax.ppermute(value, "section", [(s, (s + steps) % count) for s in range(count)])


def body(latent, cotangent, w_a, w_b, w_c, gain, tiles, pair_source, live_pairs):
    section = lax.axis_index("section")

    (w_own,) = call(
        weights_kernel,
        [((W_ROWS, H), BF16)],
        [HBM] * 4,
        [pltpu.VMEM((1, H), F32), pltpu.SemaphoreType.DMA((4,))],
        WGT_MIB,
        "weights",
    )(w_a, w_b, w_c, gain)
    w_m = around(w_own)
    (own,) = call(
        prepare_kernel,
        [((B, WIDE + H), BF16)],
        [HBM] * 5,
        [
            pltpu.VMEM((B, H), BF16), pltpu.VMEM((B, H), BF16), pltpu.VMEM(tiles.shape, BF16),
            pltpu.SMEM(pair_source.shape, jnp.int32), pltpu.SMEM(live_pairs.shape, jnp.int32),
            pltpu.SemaphoreType.DMA((5,)),
        ],
        4,
        "prepare",
    )(pair_source, live_pairs, latent, cotangent, tiles)
    first, near, value = call(
        pack_kernel,
        [((PAIR, AT3), BF16), ((PAIR, WIDE), BF16), ((PAIR, H), BF16)],
        [VMEM] * 2,
        [],
        4,
        "pack",
    )(own, swap(own))
    m1, m3, m4 = spread(first, 1), spread(near, 3), spread(value, 4)
    joined, near = call(
        join_kernel,
        [((PAIR, AT4 + H), BF16), ((PAIR, WIDE), BF16)],
        [VMEM] * 3,
        [],
        4,
        "join",
    )(m1, m3, m4)
    arrived, m4 = lax.optimization_barrier((w_m, m4))
    (w_half,) = call(half_kernel, [((W_HALF, H), BF16)], [VMEM], [], 4, "half")(arrived)
    w_mh = around(w_half)
    m2 = spread(near, 1)
    w_m, joined = lax.optimization_barrier((w_m, joined))
    joined, w_t = swap(joined), swap(w_m)
    t2, w_th = swap(m2), swap(w_mh)

    span = 2 * REACH + 1
    l0, l1, l2, l3, grad_pre, turned, v3, v2, v1, f2, f1, f0, weights = call(
        forward_kernel,
        [
            ((B, H), BF16), ((B, H), BF16), ((B, H), BF16), ((B, H), BF16),
            ((PAIR, H), BF16), ((3 * PAIR, BAND), BF16),
            ((3 * PAIR, H), BF16), ((PAIR, H), BF16), ((3 * PAIR, H), BF16),
            ((3 * PAIR, H), BF16), ((5 * PAIR, H), BF16), ((3 * PAIR, H), BF16),
            ((4 * W_ROWS, H), BF16),
        ],
        [VMEM] * 12,
        [
            pltpu.VMEM((4, B, H), BF16),
            pltpu.VMEM((span * PAIR, H), BF16), pltpu.VMEM((span * PAIR, H), BF16),
            pltpu.VMEM(((span - 2) * PAIR, BAND), BF16),
            pltpu.VMEM((span * PAIR, H), BF16), pltpu.VMEM((span * PAIR, H), BF16),
        ],
        FWD_MIB,
        "forward",
        units=160,
    )(first, m1, m2, m3, m4, joined, t2, w_own, w_m, w_t, w_mh, w_th)

    r1 = spread(grad_pre, 1)
    r2 = spread(grad_pre, 2)
    l2, r2 = lax.optimization_barrier((onward(l2, 2), r2))
    kept = [turned, v1, f1, f0, weights]
    g3, g2, turned, v1, f1, f0, weights = call(
        backward_a_kernel,
        [((B, H), BF16), ((PAIR, H), BF16)] + [(k.shape, k.dtype) for k in kept],
        [VMEM] * 12 + [ANY] * 3 + [VMEM],
        [
            pltpu.VMEM((5 * PAIR, H), BF16), pltpu.VMEM((3 * PAIR, H), BF16),
            pltpu.VMEM((3 * PAIR, H), BF16), pltpu.VMEM((3 * PAIR, H), BF16),
        ],
        BWD_MIB,
        "backward_a",
        out_specs=[VMEM] * 2 + [ANY] * len(kept),
        aliases={11 + i: 2 + i for i in range(len(kept))},
        units=60,
    )(grad_pre, r1, r2, swap(r1), swap(r2), first, m1, joined, v3, v2, f2, *kept)

    r1 = spread(g2, 1)
    r2 = spread(g2, 2)
    l1, l3, r2 = lax.optimization_barrier((onward(l1, 1), onward(l3, 3), r2))
    grads = call(
        backward_b_kernel,
        [((B, H), BF16)] * 4,
        [VMEM] * 12,
        [
            pltpu.VMEM((4, B, H), BF16),
            pltpu.VMEM((5 * PAIR, H), BF16), pltpu.VMEM((5 * PAIR, H), BF16),
            pltpu.VMEM((3 * PAIR, H), BF16), pltpu.VMEM((3 * PAIR, H), BF16),
        ],
        BWD_MIB,
        "backward_b",
        units=70,
    )(g2, r1, r2, swap(r1), swap(r2), g3, turned, v1, first, f1, f0, weights)

    moved = [onward(piece, step) for step, piece in enumerate(grads) if step]
    latent_result, grad_result = call(
        collect_kernel,
        [((4, B, H), BF16)] * 2,
        [VMEM] * 8,
        [pltpu.SemaphoreType.DMA((8,))],
        4,
        "collect",
        out_specs=[HBM] * 2,
    )(l0, l1, l2, l3, grads[0], *moved)
    return (latent_result[None], grad_result[None])


def solution(mesh):
    devices = np.asarray(mesh.devices)
    sections, parts = devices.shape
    split = Mesh(devices.reshape(sections, parts // 2, 2), ("section", "chip", "core"))
    dom = ("chip", "core")
    in_specs = (
        P(None, dom, None),
        P(None, dom, None),
        P("section", None, None),
        P("section", None, None),
        P("section", None, None),
        P("section", None),
        P(dom, None, None),
        P(dom),
        P(dom),
    )
    out_specs = (P("section", None, dom, None), P("section", None, dom, None))
    return jax.shard_map(body, mesh=split, in_specs=in_specs, out_specs=out_specs, check_vma=False)
```

```python
import functools

import jax
import jax.numpy as jnp
import numpy as np
from jax import lax
from jax.experimental import pallas as pl
from jax.experimental.pallas import tpu as pltpu
from jax.sharding import Mesh, PartitionSpec as P

EPS = 1e-05
H = 512
B = 128
PAIR = 2 * B
BAND = 3 * PAIR
SENT = 5 * B
WIDE = H + SENT
AT2 = WIDE + H
AT3 = AT2 + WIDE
AT4 = AT3 + WIDE
REACH = 4
W_ROWS = 3 * H + 32
W_HALF = W_ROWS // 2
F32, BF16 = jnp.float32, jnp.bfloat16
VMEM = pl.BlockSpec(memory_space=pltpu.VMEM)
HBM = pl.BlockSpec(memory_space=pltpu.HBM)
ANY = pl.BlockSpec(memory_space=pl.ANY)
FWD_MIB, BWD_MIB, WGT_MIB = 24, 12, 58


def rows(index, size=PAIR):
    if isinstance(index, int):
        return pl.ds(index * size, size)
    return pl.ds(pl.multiple_of(index * size, size), size)


def dot(a, b):
    return jnp.dot(a, b, preferred_element_type=F32)


def dot_t(a, b):
    return lax.dot_general(a, b, (((1,), (1,)), ((), ())), preferred_element_type=F32)


def normed_rows(values):
    wide = values.astype(F32)
    centre = wide - jnp.mean(wide, axis=-1, keepdims=True)
    inv = lax.rsqrt(jnp.mean(centre * centre, axis=-1, keepdims=True) + EPS)
    return centre * inv, inv


def call(kernel, outs, specs, scratch, limit_mib, name, out_specs=None, aliases=None, units=0):
    return pl.pallas_call(
        kernel,
        out_shape=[jax.ShapeDtypeStruct(s, d) for s, d in outs],
        in_specs=specs,
        out_specs=out_specs or [VMEM] * len(outs),
        input_output_aliases=aliases or {},
        cost_estimate=pl.CostEstimate(
            flops=units * 2 * B * H * H, bytes_accessed=units * 2 * B * H, transcendentals=0
        ),
        scratch_shapes=scratch,
        compiler_params=pltpu.CompilerParams(vmem_limit_bytes=limit_mib << 20),
        name=name,
    )


def weights_kernel(w_a, w_b, w_c, gain, weights, gain_here, sems):
    copies = [
        pltpu.make_async_copy(ref.at[0], weights.at[rows(which, H)], sems.at[which])
        for which, ref in enumerate((w_a, w_b, w_c))
    ]
    first = pltpu.make_async_copy(gain, gain_here, sems.at[3])
    first.start()
    for copy in copies:
        copy.start()
    first.wait()
    rest = jnp.broadcast_to(gain_here[0:1, :], (32, H))
    high = rest.astype(BF16).astype(F32)
    rest = rest - high
    mid = rest.astype(BF16).astype(F32)
    low = rest - mid
    row = lax.broadcasted_iota(jnp.int32, (32, H), 0)
    held = jnp.where(row == 0, high, jnp.where(row == 1, mid, jnp.where(row == 2, low, 0.0)))
    weights[3 * H : 3 * H + 32, :] = held.astype(BF16)
    for copy in copies:
        copy.wait()


def half_kernel(weights, half):
    core = lax.axis_index("core")
    half[...] = weights[pl.ds(pl.multiple_of(core * W_HALF, 16), W_HALF), :]


def prepare_kernel(source, live, latent, cotangent, tiles, own, value, slope, tile, index, count, sems):
    sample = lax.axis_index("section")
    copies = [
        pltpu.make_async_copy(tiles, tile, sems.at[0]),
        pltpu.make_async_copy(source, index, sems.at[1]),
        pltpu.make_async_copy(live, count, sems.at[2]),
        pltpu.make_async_copy(latent.at[sample], value, sems.at[3]),
        pltpu.make_async_copy(cotangent.at[sample], slope, sems.at[4]),
    ]
    for copy in copies:
        copy.start()
    for copy in copies[:3]:
        copy.wait()
    slots = tile.shape[0]
    base = 2 * lax.axis_index("chip") + lax.axis_index("core") - 2
    for column in range(5):
        total = jnp.zeros((B, B), F32)
        for slot in range(slots):
            hit = (index[slot] - base == column) & (slot < count[0])
            total = total + jnp.where(hit, tile[slot].astype(F32), 0.0)
        own[:, H + column * B : H + (column + 1) * B] = total.astype(BF16)
    for copy in copies[3:]:
        copy.wait()
    own[:, 0:H] = value[...]
    own[:, WIDE:] = slope[...]


def pack_kernel(own, partner, first, near, value):
    core = lax.axis_index("core")
    for ref, held in ((own, core), (partner, 1 - core)):
        first[rows(held, B), :] = ref[...]
        near[rows(held, B), :] = ref[:, 0:WIDE]
        value[rows(held, B), :] = ref[:, 0:H]


def cut_kernel(m1, _, near):
    near[...] = m1[:, 0:WIDE]


def join_kernel(m1, m2, m3, m4, _, __, joined):
    joined[:, 0:AT2] = m1[...]
    joined[:, AT2:AT3] = m2[...]
    joined[:, AT3:AT4] = m3[...]
    joined[:, AT4:] = m4[...]


def layer_gain(weights, layer):
    terms = weights[layer * W_ROWS + 3 * H : layer * W_ROWS + 3 * H + 16, :].astype(F32)
    return jnp.sum(terms, axis=0, keepdims=True)


def weight(weights, layer, which):
    start = layer * W_ROWS + which * H
    return weights[start : start + H, :]


def forward_kernel(
    own, m1, m2, m3, m4, joined, w_own, w_m, w_t, w_mh, w_th,
    latents, grad_pre, turned, v3_out, v2_out, v1_out, f2_out, f1_out, f0_out, weights,
    v_a, v_b, band, unit, source,
):
    section, core = lax.axis_index("section"), lax.axis_index("core")
    weights[pl.ds(pl.multiple_of(section * W_ROWS, 16), W_ROWS), :] = w_own[...]
    before, after = (section + 3) % 4, (section + 1) % 4
    mine = jnp.where(core == 0, before, after)
    theirs = jnp.where(core == 0, after, before)
    far = (section + 2) % 4
    weights[pl.ds(pl.multiple_of(mine * W_ROWS, 16), W_ROWS), :] = w_m[...]
    weights[pl.ds(pl.multiple_of(theirs * W_ROWS, 16), W_ROWS), :] = w_t[...]
    weights[pl.ds(pl.multiple_of(far * W_ROWS + core * W_HALF, 16), W_HALF), :] = w_mh[...]
    weights[pl.ds(pl.multiple_of(far * W_ROWS + (1 - core) * W_HALF, 16), W_HALF), :] = w_th[...]

    def put_band(at, ref):
        for k in range(2):
            row = pl.ds(pl.multiple_of(at * PAIR + k * B, B), B)
            band[row, k * B : k * B + SENT] = ref[k * B : (k + 1) * B, H:WIDE]
            rim = (1 - k) * SENT
            band[row, rim : rim + B] = jnp.zeros((B, B), BF16)

    t1, t2 = joined.at[:, 0:AT2], joined.at[:, AT2:AT3]
    t3, t4 = joined.at[:, AT3:AT4], joined.at[:, AT4:]
    v_a[rows(REACH), :] = own[:, 0:H]
    put_band(REACH - 1, own)
    for step, (m, t) in enumerate(((m1, t1), (m2, t2), (m3, t3), (m4, t4)), start=1):
        at_m = REACH - step + 2 * step * core
        at_t = 2 * REACH - at_m
        v_a[rows(at_m), :] = m[:, 0:H]
        v_a[rows(at_t), :] = t[:, 0:H]
        if step < REACH:
            put_band(at_m - 1, m)
            put_band(at_t - 1, t)

    now, later = v_a, v_b
    for layer in range(4):
        low, high = layer, 2 * REACH - layer
        gain = layer_gain(weights, layer)

        def project(j):
            value, _ = normed_rows(now[rows(j), :])
            held = (value * gain).astype(BF16)
            unit[rows(j), :] = held
            source[rows(j), :] = dot(held, weight(weights, layer, 0)).astype(BF16)

        def update(j):
            pre = dot(band[rows(j - 1), :], source[(j - 1) * PAIR : (j - 1) * PAIR + BAND, :])
            pre = pre + dot(unit[rows(j), :], weight(weights, layer, 1))
            sigma = 0.5 + 0.5 * jnp.tanh(0.5 * pre)
            act = (pre * sigma).astype(BF16)
            value = now[rows(j), :].astype(F32) + dot(act, weight(weights, layer, 2))
            later[rows(j), :] = value.astype(BF16)
            reach = (1, 2, 1, 0)[layer]
            if abs(j - REACH) <= reach:
                factor = sigma * (1.0 + pre * (1.0 - sigma))
                if layer == 3:
                    incoming = dot_t(own[:, WIDE:], weight(weights, 3, 2))
                    grad_pre[...] = (incoming * factor).astype(BF16)
                else:
                    out = (f0_out, f1_out, f2_out)[layer]
                    out[rows(j - REACH + reach), :] = factor.astype(BF16)

        for j in range(low, low + 3):
            project(j)
        for j in range(low + 1, high):
            update(j)
            if j + 2 <= high:
                project(j + 2)
        latents[layer] = later[pl.ds(pl.multiple_of(REACH * PAIR + core * B, B), B), :]
        if layer == 0:
            v1_out[...] = later[3 * PAIR : 6 * PAIR, :]
        if layer == 1:
            v2_out[...] = later[4 * PAIR : 5 * PAIR, :]
        if layer == 2:
            v3_out[...] = later[3 * PAIR : 6 * PAIR, :]
        now, later = later, now

    for j in range(3, 6):
        for i in range(j - 1, j + 2):
            column = (j - i + 1) * PAIR
            piece = band[(i - 1) * PAIR : i * PAIR, column : column + PAIR]
            turned[(j - 3) * PAIR : (j - 2) * PAIR, (i - j + 1) * PAIR : (i - j + 2) * PAIR] = (
                piece.astype(F32).T.astype(BF16)
            )


def grad_pair(gradient, grad_pre, window, turned, values, weights, layer):
    back = dot(turned, window).astype(BF16)
    grad_unit = dot_t(grad_pre, weight(weights, layer, 1))
    grad_unit = grad_unit + dot_t(back, weight(weights, layer, 0))
    normed, inv = normed_rows(values)
    e = grad_unit * layer_gain(weights, layer)
    grad_in = inv * (
        e
        - jnp.mean(e, axis=-1, keepdims=True)
        - normed * jnp.mean(e * normed, axis=-1, keepdims=True)
    )
    return (gradient.astype(F32) + grad_in).astype(BF16)


def place(target, own, sides, core):
    middle = len(sides)
    target[rows(middle), :] = own[...]
    for step, (mine, theirs) in enumerate(sides, start=1):
        at_m = middle - step + 2 * step * core
        target[rows(at_m), :] = mine[...]
        target[rows(2 * middle - at_m), :] = theirs[...]


def backward_a_kernel(
    grad_pre, r1, r2, o1, o2, own, m1, t1, v3, v2, f2, turned, v1, f1, f0, latents, weights,
    g3_out, g2_out, kept_turned, kept_v1, kept_f1, kept_f0, kept_latents, kept_weights, held, cot, g3, gp2,
):
    core = lax.axis_index("core")
    place(held, grad_pre, ((r1, o1), (r2, o2)), core)
    place(cot, own.at[:, WIDE:], ((m1.at[:, WIDE:], t1.at[:, WIDE:AT2]),), core)
    for j in range(3):
        g3[rows(j), :] = grad_pair(
            cot[rows(j), :], held[rows(j + 1), :], held[j * PAIR : j * PAIR + BAND, :],
            turned[rows(j), :], v3[rows(j), :], weights, 3,
        )
        gp2[rows(j), :] = (dot_t(g3[rows(j), :], weight(weights, 2, 2)) * f2[rows(j), :]).astype(BF16)
    g3_out[...] = g3[pl.ds(pl.multiple_of(PAIR + core * B, B), B), :]
    g2_out[...] = grad_pair(
        g3[rows(1), :], gp2[rows(1), :], gp2[...], turned[rows(1), :], v2[...], weights, 2
    )


def backward_b_kernel(
    g2_own, r1, r2, o1, o2, g3_mine, turned, v1, own, f1, f0, latents, weights,
    results, g2, gp1, g1, gp0,
):
    core = lax.axis_index("core")
    place(g2, g2_own, ((r1, o1), (r2, o2)), core)
    for j in range(5):
        gp1[rows(j), :] = (dot_t(g2[rows(j), :], weight(weights, 1, 2)) * f1[rows(j), :]).astype(BF16)
    for j in range(3):
        g1[rows(j), :] = grad_pair(
            g2[rows(j + 1), :], gp1[rows(j + 1), :], gp1[j * PAIR : j * PAIR + BAND, :],
            turned[rows(j), :], v1[rows(j), :], weights, 1,
        )
        gp0[rows(j), :] = (dot_t(g1[rows(j), :], weight(weights, 0, 2)) * f0[rows(j), :]).astype(BF16)
    mine = pl.ds(pl.multiple_of(PAIR + core * B, B), B)
    results[:, 0:B, :] = latents[...]
    results[3, B:PAIR, :] = g3_mine[...]
    results[2, B:PAIR, :] = g2_own[rows(core, B), :]
    results[1, B:PAIR, :] = g1[mine, :]
    g0 = grad_pair(g1[rows(1), :], gp0[rows(1), :], gp0[...], turned[rows(1), :], own[:, 0:H], weights, 0)
    g1[rows(1), :] = g0
    results[0, B:PAIR, :] = g1[mine, :]


def split_kernel(results, latents, grads, sems):
    copies = [
        pltpu.make_async_copy(results.at[:, pl.ds(0, B)], latents, sems.at[0]),
        pltpu.make_async_copy(results.at[:, pl.ds(B, B)], grads, sems.at[1]),
    ]
    for copy in copies:
        copy.start()
    for copy in copies:
        copy.wait()


def swap(value):
    return lax.ppermute(value, "core", [(0, 1), (1, 0)])


def spread(value, steps):
    chips = lax.axis_size("chip")
    pairs = []
    for c in range(chips):
        if c + steps < chips:
            pairs.append((2 * c, 2 * (c + steps)))
        if c - steps >= 0:
            pairs.append((2 * c + 1, 2 * (c - steps) + 1))
    return lax.ppermute(value, ("chip", "core"), pairs)


def around(value):
    count = lax.axis_size("section")
    pairs = []
    for s in range(count):
        pairs.append((2 * s, 2 * ((s + 1) % count)))
        pairs.append((2 * s + 1, 2 * ((s - 1) % count) + 1))
    return lax.ppermute(value, ("section", "core"), pairs)


def body(latent, cotangent, w_a, w_b, w_c, gain, tiles, pair_source, live_pairs):
    section = lax.axis_index("section")

    (w_own,) = call(
        weights_kernel,
        [((W_ROWS, H), BF16)],
        [HBM] * 4,
        [pltpu.VMEM((1, H), F32), pltpu.SemaphoreType.DMA((4,))],
        WGT_MIB,
        "weights",
    )(w_a, w_b, w_c, gain)
    w_m = around(w_own)
    (own,) = call(
        prepare_kernel,
        [((B, WIDE + H), BF16)],
        [HBM] * 5,
        [
            pltpu.VMEM((B, H), BF16), pltpu.VMEM((B, H), BF16), pltpu.VMEM(tiles.shape, BF16),
            pltpu.SMEM(pair_source.shape, jnp.int32), pltpu.SMEM(live_pairs.shape, jnp.int32),
            pltpu.SemaphoreType.DMA((5,)),
        ],
        4,
        "prepare",
    )(pair_source, live_pairs, latent, cotangent, tiles)
    first, near, value = call(
        pack_kernel,
        [((PAIR, AT2), BF16), ((PAIR, WIDE), BF16), ((PAIR, H), BF16)],
        [VMEM] * 2,
        [],
        4,
        "pack",
    )(own, swap(own))
    m1, m3, m4 = spread(first, 1), spread(near, 3), spread(value, 4)
    arrived, m4 = lax.optimization_barrier((w_m, m4))
    (w_half,) = call(half_kernel, [((W_HALF, H), BF16)], [VMEM], [], 4, "half")(arrived)
    w_mh = around(w_half)
    (near,) = call(cut_kernel, [((PAIR, WIDE), BF16)], [VMEM, ANY], [], 4, "cut")(m1, w_half)
    m2 = spread(near, 1)
    w_t = swap(w_m)
    (joined,) = call(
        join_kernel, [((PAIR, AT4 + H), BF16)], [VMEM] * 4 + [ANY] * 2, [], 4, "join"
    )(m1, m2, m3, m4, w_mh, w_t)
    joined, w_th = swap(joined), swap(w_mh)

    span = 2 * REACH + 1
    latents, grad_pre, turned, v3, v2, v1, f2, f1, f0, weights = call(
        forward_kernel,
        [
            ((4, B, H), BF16), ((PAIR, H), BF16), ((3 * PAIR, BAND), BF16),
            ((3 * PAIR, H), BF16), ((PAIR, H), BF16), ((3 * PAIR, H), BF16),
            ((3 * PAIR, H), BF16), ((5 * PAIR, H), BF16), ((3 * PAIR, H), BF16),
            ((4 * W_ROWS, H), BF16),
        ],
        [VMEM] * 11,
        [
            pltpu.VMEM((span * PAIR, H), BF16), pltpu.VMEM((span * PAIR, H), BF16),
            pltpu.VMEM(((span - 2) * PAIR, BAND), BF16),
            pltpu.VMEM((span * PAIR, H), BF16), pltpu.VMEM((span * PAIR, H), BF16),
        ],
        FWD_MIB,
        "forward",
        units=160,
    )(first, m1, m2, m3, m4, joined, w_own, w_m, w_t, w_mh, w_th)

    r1 = spread(grad_pre, 1)
    r2 = spread(grad_pre, 2)
    kept = [turned, v1, f1, f0, latents, weights]
    g3, g2, turned, v1, f1, f0, latents, weights = call(
        backward_a_kernel,
        [((B, H), BF16), ((PAIR, H), BF16)] + [(k.shape, k.dtype) for k in kept],
        [VMEM] * 12 + [ANY] * 4 + [VMEM],
        [
            pltpu.VMEM((5 * PAIR, H), BF16), pltpu.VMEM((3 * PAIR, H), BF16),
            pltpu.VMEM((3 * PAIR, H), BF16), pltpu.VMEM((3 * PAIR, H), BF16),
        ],
        BWD_MIB,
        "backward_a",
        out_specs=[VMEM] * 2 + [ANY] * len(kept),
        aliases={11 + i: 2 + i for i in range(len(kept))},
        units=60,
    )(grad_pre, r1, r2, swap(r1), swap(r2), first, m1, joined, v3, v2, f2, *kept)

    r1 = spread(g2, 1)
    r2 = spread(g2, 2)
    (results,) = call(
        backward_b_kernel,
        [((4, PAIR, H), BF16)],
        [VMEM] * 13,
        [
            pltpu.VMEM((5 * PAIR, H), BF16), pltpu.VMEM((5 * PAIR, H), BF16),
            pltpu.VMEM((3 * PAIR, H), BF16), pltpu.VMEM((3 * PAIR, H), BF16),
        ],
        BWD_MIB,
        "backward_b",
        units=70,
    )(g2, r1, r2, swap(r1), swap(r2), g3, turned, v1, first, f1, f0, latents, weights)

    results = lax.all_to_all(results, "section", 0, 0, tiled=True)
    latent_result, grad_result = call(
        split_kernel,
        [((4, B, H), BF16)] * 2,
        [ANY],
        [pltpu.SemaphoreType.DMA((2,))],
        4,
        "split",
        out_specs=[HBM] * 2,
    )(results)
    return (latent_result[None], grad_result[None])


def solution(mesh):
    devices = np.asarray(mesh.devices)
    sections, parts = devices.shape
    split = Mesh(devices.reshape(sections, parts // 2, 2), ("section", "chip", "core"))
    dom = ("chip", "core")
    in_specs = (
        P(None, dom, None),
        P(None, dom, None),
        P("section", None, None),
        P("section", None, None),
        P("section", None, None),
        P("section", None),
        P(dom, None, None),
        P(dom),
        P(dom),
    )
    out_specs = (P("section", None, dom, None), P("section", None, dom, None))
    return jax.shard_map(body, mesh=split, in_specs=in_specs, out_specs=out_specs, check_vma=False)
```

```python
import functools

import jax
import jax.numpy as jnp
import numpy as np
from jax import lax
from jax.experimental import pallas as pl
from jax.experimental.pallas import tpu as pltpu
from jax.sharding import Mesh, PartitionSpec as P

EPS = 1e-05
H = 512
B = 128
PAIR = 2 * B
BAND = 3 * PAIR
SENT = 5 * B
WIDE = H + SENT
AT2 = WIDE + H
AT3 = AT2 + WIDE
AT4 = AT3 + WIDE
REACH = 4
W_ROWS = 3 * H + 32
W_HALF = W_ROWS // 2
F32, BF16 = jnp.float32, jnp.bfloat16
VMEM = pl.BlockSpec(memory_space=pltpu.VMEM)
HBM = pl.BlockSpec(memory_space=pltpu.HBM)
ANY = pl.BlockSpec(memory_space=pl.ANY)
FWD_MIB, BWD_MIB, WGT_MIB = 24, 12, 58


def rows(index, size=PAIR):
    if isinstance(index, int):
        return pl.ds(index * size, size)
    return pl.ds(pl.multiple_of(index * size, size), size)


def dot(a, b):
    return jnp.dot(a, b, preferred_element_type=F32)


def dot_t(a, b):
    return lax.dot_general(a, b, (((1,), (1,)), ((), ())), preferred_element_type=F32)


def normed_rows(values):
    wide = values.astype(F32)
    centre = wide - jnp.mean(wide, axis=-1, keepdims=True)
    inv = lax.rsqrt(jnp.mean(centre * centre, axis=-1, keepdims=True) + EPS)
    return centre * inv, inv


def call(kernel, outs, specs, scratch, limit_mib, name, out_specs=None, aliases=None, units=0):
    return pl.pallas_call(
        kernel,
        out_shape=[jax.ShapeDtypeStruct(s, d) for s, d in outs],
        in_specs=specs,
        out_specs=out_specs or [VMEM] * len(outs),
        input_output_aliases=aliases or {},
        cost_estimate=pl.CostEstimate(
            flops=units * 2 * B * H * H, bytes_accessed=units * 2 * B * H, transcendentals=0
        ),
        scratch_shapes=scratch,
        compiler_params=pltpu.CompilerParams(vmem_limit_bytes=limit_mib << 20),
        name=name,
    )


def weights_kernel(w_a, w_b, w_c, gain, weights, gain_here, sems):
    copies = [
        pltpu.make_async_copy(ref.at[0], weights.at[rows(which, H)], sems.at[which])
        for which, ref in enumerate((w_a, w_b, w_c))
    ]
    first = pltpu.make_async_copy(gain, gain_here, sems.at[3])
    first.start()
    for copy in copies:
        copy.start()
    first.wait()
    rest = jnp.broadcast_to(gain_here[0:1, :], (32, H))
    high = rest.astype(BF16).astype(F32)
    rest = rest - high
    mid = rest.astype(BF16).astype(F32)
    low = rest - mid
    row = lax.broadcasted_iota(jnp.int32, (32, H), 0)
    held = jnp.where(row == 0, high, jnp.where(row == 1, mid, jnp.where(row == 2, low, 0.0)))
    weights[3 * H : 3 * H + 32, :] = held.astype(BF16)
    for copy in copies:
        copy.wait()


def half_kernel(weights, half):
    core = lax.axis_index("core")
    half[...] = weights[pl.ds(pl.multiple_of(core * W_HALF, 16), W_HALF), :]


def prepare_kernel(source, live, latent, cotangent, tiles, own, value, slope, tile, index, count, sems):
    sample = lax.axis_index("section")
    copies = [
        pltpu.make_async_copy(tiles, tile, sems.at[0]),
        pltpu.make_async_copy(source, index, sems.at[1]),
        pltpu.make_async_copy(live, count, sems.at[2]),
        pltpu.make_async_copy(latent.at[sample], value, sems.at[3]),
        pltpu.make_async_copy(cotangent.at[sample], slope, sems.at[4]),
    ]
    for copy in copies:
        copy.start()
    for copy in copies[:3]:
        copy.wait()
    slots = tile.shape[0]
    base = 2 * lax.axis_index("chip") + lax.axis_index("core") - 2
    for column in range(5):
        total = jnp.zeros((B, B), F32)
        for slot in range(slots):
            hit = (index[slot] - base == column) & (slot < count[0])
            total = total + jnp.where(hit, tile[slot].astype(F32), 0.0)
        own[:, H + column * B : H + (column + 1) * B] = total.astype(BF16)
    for copy in copies[3:]:
        copy.wait()
    own[:, 0:H] = value[...]
    own[:, WIDE:] = slope[...]


def pack_kernel(own, partner, first, near, value):
    core = lax.axis_index("core")
    for ref, held in ((own, core), (partner, 1 - core)):
        first[rows(held, B), :] = ref[...]
        near[rows(held, B), :] = ref[:, 0:WIDE]
        value[rows(held, B), :] = ref[:, 0:H]


def cut_kernel(m1, _, __, near):
    near[...] = m1[:, 0:WIDE]


def join_kernel(m1, m2, m3, m4, _, __, joined):
    joined[:, 0:AT2] = m1[...]
    joined[:, AT2:AT3] = m2[...]
    joined[:, AT3:AT4] = m3[...]
    joined[:, AT4:] = m4[...]


def layer_gain(weights, layer):
    terms = weights[layer * W_ROWS + 3 * H : layer * W_ROWS + 3 * H + 16, :].astype(F32)
    return jnp.sum(terms, axis=0, keepdims=True)


def weight(weights, layer, which):
    start = layer * W_ROWS + which * H
    return weights[start : start + H, :]


def forward_kernel(
    own, m1, m2, m3, m4, joined, w_own, w_m, w_t, w_mh, w_th,
    latents, grad_pre, turned, v3_out, v2_out, v1_out, f2_out, f1_out, f0_out, weights,
    v_a, v_b, band, unit, source,
):
    section, core = lax.axis_index("section"), lax.axis_index("core")
    weights[pl.ds(pl.multiple_of(section * W_ROWS, 16), W_ROWS), :] = w_own[...]
    before, after = (section + 3) % 4, (section + 1) % 4
    mine = jnp.where(core == 0, before, after)
    theirs = jnp.where(core == 0, after, before)
    far = (section + 2) % 4
    weights[pl.ds(pl.multiple_of(mine * W_ROWS, 16), W_ROWS), :] = w_m[...]
    weights[pl.ds(pl.multiple_of(theirs * W_ROWS, 16), W_ROWS), :] = w_t[...]
    weights[pl.ds(pl.multiple_of(far * W_ROWS + core * W_HALF, 16), W_HALF), :] = w_mh[...]
    weights[pl.ds(pl.multiple_of(far * W_ROWS + (1 - core) * W_HALF, 16), W_HALF), :] = w_th[...]

    def put_band(at, ref):
        for k in range(2):
            row = pl.ds(pl.multiple_of(at * PAIR + k * B, B), B)
            band[row, k * B : k * B + SENT] = ref[k * B : (k + 1) * B, H:WIDE]
            rim = (1 - k) * SENT
            band[row, rim : rim + B] = jnp.zeros((B, B), BF16)

    t1, t2 = joined.at[:, 0:AT2], joined.at[:, AT2:AT3]
    t3, t4 = joined.at[:, AT3:AT4], joined.at[:, AT4:]
    v_a[rows(REACH), :] = own[:, 0:H]
    put_band(REACH - 1, own)
    for step, (m, t) in enumerate(((m1, t1), (m2, t2), (m3, t3), (m4, t4)), start=1):
        at_m = REACH - step + 2 * step * core
        at_t = 2 * REACH - at_m
        v_a[rows(at_m), :] = m[:, 0:H]
        v_a[rows(at_t), :] = t[:, 0:H]
        if step < REACH:
            put_band(at_m - 1, m)
            put_band(at_t - 1, t)

    now, later = v_a, v_b
    for layer in range(4):
        low, high = layer, 2 * REACH - layer
        gain = layer_gain(weights, layer)

        def project(j):
            value, _ = normed_rows(now[rows(j), :])
            held = (value * gain).astype(BF16)
            unit[rows(j), :] = held
            source[rows(j), :] = dot(held, weight(weights, layer, 0)).astype(BF16)

        def update(j):
            pre = dot(band[rows(j - 1), :], source[(j - 1) * PAIR : (j - 1) * PAIR + BAND, :])
            pre = pre + dot(unit[rows(j), :], weight(weights, layer, 1))
            sigma = 0.5 + 0.5 * jnp.tanh(0.5 * pre)
            act = (pre * sigma).astype(BF16)
            value = now[rows(j), :].astype(F32) + dot(act, weight(weights, layer, 2))
            later[rows(j), :] = value.astype(BF16)
            reach = (1, 2, 1, 0)[layer]
            if abs(j - REACH) <= reach:
                factor = sigma * (1.0 + pre * (1.0 - sigma))
                if layer == 3:
                    incoming = dot_t(own[:, WIDE:], weight(weights, 3, 2))
                    grad_pre[...] = (incoming * factor).astype(BF16)
                else:
                    out = (f0_out, f1_out, f2_out)[layer]
                    out[rows(j - REACH + reach), :] = factor.astype(BF16)

        for j in range(low, low + 3):
            project(j)
        for j in range(low + 1, high):
            update(j)
            if j + 2 <= high:
                project(j + 2)
        latents[layer] = later[pl.ds(pl.multiple_of(REACH * PAIR + core * B, B), B), :]
        if layer == 0:
            v1_out[...] = later[3 * PAIR : 6 * PAIR, :]
        if layer == 1:
            v2_out[...] = later[4 * PAIR : 5 * PAIR, :]
        if layer == 2:
            v3_out[...] = later[3 * PAIR : 6 * PAIR, :]
        now, later = later, now

    for j in range(3, 6):
        for i in range(j - 1, j + 2):
            column = (j - i + 1) * PAIR
            piece = band[(i - 1) * PAIR : i * PAIR, column : column + PAIR]
            turned[(j - 3) * PAIR : (j - 2) * PAIR, (i - j + 1) * PAIR : (i - j + 2) * PAIR] = (
                piece.astype(F32).T.astype(BF16)
            )


def grad_pair(gradient, grad_pre, window, turned, values, weights, layer):
    back = dot(turned, window).astype(BF16)
    grad_unit = dot_t(grad_pre, weight(weights, layer, 1))
    grad_unit = grad_unit + dot_t(back, weight(weights, layer, 0))
    normed, inv = normed_rows(values)
    e = grad_unit * layer_gain(weights, layer)
    grad_in = inv * (
        e
        - jnp.mean(e, axis=-1, keepdims=True)
        - normed * jnp.mean(e * normed, axis=-1, keepdims=True)
    )
    return (gradient.astype(F32) + grad_in).astype(BF16)


def place(target, own, sides, core):
    middle = len(sides)
    target[rows(middle), :] = own[...]
    for step, (mine, theirs) in enumerate(sides, start=1):
        at_m = middle - step + 2 * step * core
        target[rows(at_m), :] = mine[...]
        target[rows(2 * middle - at_m), :] = theirs[...]


def backward_a_kernel(
    grad_pre, r1, r2, o1, o2, own, m1, t1, v3, v2, f2, turned, v1, f1, f0, latents, weights,
    g3_out, g2_out, kept_turned, kept_v1, kept_f1, kept_f0, kept_latents, kept_weights, held, cot, g3, gp2,
):
    core = lax.axis_index("core")
    place(held, grad_pre, ((r1, o1), (r2, o2)), core)
    place(cot, own.at[:, WIDE:], ((m1.at[:, WIDE:], t1.at[:, WIDE:AT2]),), core)
    for j in range(3):
        g3[rows(j), :] = grad_pair(
            cot[rows(j), :], held[rows(j + 1), :], held[j * PAIR : j * PAIR + BAND, :],
            turned[rows(j), :], v3[rows(j), :], weights, 3,
        )
        gp2[rows(j), :] = (dot_t(g3[rows(j), :], weight(weights, 2, 2)) * f2[rows(j), :]).astype(BF16)
    g3_out[...] = g3[pl.ds(pl.multiple_of(PAIR + core * B, B), B), :]
    g2_out[...] = grad_pair(
        g3[rows(1), :], gp2[rows(1), :], gp2[...], turned[rows(1), :], v2[...], weights, 2
    )


def backward_b_kernel(
    g2_own, r1, r2, o1, o2, g3_mine, turned, v1, own, f1, f0, latents, weights,
    results, g2, gp1, g1, gp0,
):
    core = lax.axis_index("core")
    place(g2, g2_own, ((r1, o1), (r2, o2)), core)
    for j in range(5):
        gp1[rows(j), :] = (dot_t(g2[rows(j), :], weight(weights, 1, 2)) * f1[rows(j), :]).astype(BF16)
    for j in range(3):
        g1[rows(j), :] = grad_pair(
            g2[rows(j + 1), :], gp1[rows(j + 1), :], gp1[j * PAIR : j * PAIR + BAND, :],
            turned[rows(j), :], v1[rows(j), :], weights, 1,
        )
        gp0[rows(j), :] = (dot_t(g1[rows(j), :], weight(weights, 0, 2)) * f0[rows(j), :]).astype(BF16)
    mine = pl.ds(pl.multiple_of(PAIR + core * B, B), B)
    results[:, 0:B, :] = latents[...]
    results[3, B:PAIR, :] = g3_mine[...]
    results[2, B:PAIR, :] = g2_own[rows(core, B), :]
    results[1, B:PAIR, :] = g1[mine, :]
    g0 = grad_pair(g1[rows(1), :], gp0[rows(1), :], gp0[...], turned[rows(1), :], own[:, 0:H], weights, 0)
    g1[rows(1), :] = g0
    results[0, B:PAIR, :] = g1[mine, :]


def split_kernel(results, latents, grads, sems):
    copies = [
        pltpu.make_async_copy(results.at[:, pl.ds(0, B)], latents, sems.at[0]),
        pltpu.make_async_copy(results.at[:, pl.ds(B, B)], grads, sems.at[1]),
    ]
    for copy in copies:
        copy.start()
    for copy in copies:
        copy.wait()


def swap(value):
    return lax.ppermute(value, "core", [(0, 1), (1, 0)])


def spread(value, steps):
    chips = lax.axis_size("chip")
    pairs = []
    for c in range(chips):
        if c + steps < chips:
            pairs.append((2 * c, 2 * (c + steps)))
        if c - steps >= 0:
            pairs.append((2 * c + 1, 2 * (c - steps) + 1))
    return lax.ppermute(value, ("chip", "core"), pairs)


def around(value):
    count = lax.axis_size("section")
    pairs = []
    for s in range(count):
        pairs.append((2 * s, 2 * ((s + 1) % count)))
        pairs.append((2 * s + 1, 2 * ((s - 1) % count) + 1))
    return lax.ppermute(value, ("section", "core"), pairs)


def body(latent, cotangent, w_a, w_b, w_c, gain, tiles, pair_source, live_pairs):
    section = lax.axis_index("section")

    (w_own,) = call(
        weights_kernel,
        [((W_ROWS, H), BF16)],
        [HBM] * 4,
        [pltpu.VMEM((1, H), F32), pltpu.SemaphoreType.DMA((4,))],
        WGT_MIB,
        "weights",
    )(w_a, w_b, w_c, gain)
    w_m = around(w_own)
    (own,) = call(
        prepare_kernel,
        [((B, WIDE + H), BF16)],
        [HBM] * 5,
        [
            pltpu.VMEM((B, H), BF16), pltpu.VMEM((B, H), BF16), pltpu.VMEM(tiles.shape, BF16),
            pltpu.SMEM(pair_source.shape, jnp.int32), pltpu.SMEM(live_pairs.shape, jnp.int32),
            pltpu.SemaphoreType.DMA((5,)),
        ],
        4,
        "prepare",
    )(pair_source, live_pairs, latent, cotangent, tiles)
    first, near, value = call(
        pack_kernel,
        [((PAIR, AT2), BF16), ((PAIR, WIDE), BF16), ((PAIR, H), BF16)],
        [VMEM] * 2,
        [],
        4,
        "pack",
    )(own, swap(own))
    m1, m3, m4 = spread(first, 1), spread(near, 3), spread(value, 4)
    arrived, m4 = lax.optimization_barrier((w_m, m4))
    (w_half,) = call(half_kernel, [((W_HALF, H), BF16)], [VMEM], [], 4, "half")(arrived)
    w_mh = around(w_half)
    (near,) = call(cut_kernel, [((PAIR, WIDE), BF16)], [VMEM, ANY, ANY], [], 4, "cut")(m1, w_half, m3)
    w_m, near = lax.optimization_barrier((w_m, near))
    m2 = spread(near, 1)
    w_t = swap(w_m)
    (joined,) = call(
        join_kernel, [((PAIR, AT4 + H), BF16)], [VMEM] * 4 + [ANY] * 2, [], 4, "join"
    )(m1, m2, m3, m4, w_mh, w_t)
    joined, w_th = swap(joined), swap(w_mh)

    span = 2 * REACH + 1
    latents, grad_pre, turned, v3, v2, v1, f2, f1, f0, weights = call(
        forward_kernel,
        [
            ((4, B, H), BF16), ((PAIR, H), BF16), ((3 * PAIR, BAND), BF16),
            ((3 * PAIR, H), BF16), ((PAIR, H), BF16), ((3 * PAIR, H), BF16),
            ((3 * PAIR, H), BF16), ((5 * PAIR, H), BF16), ((3 * PAIR, H), BF16),
            ((4 * W_ROWS, H), BF16),
        ],
        [VMEM] * 11,
        [
            pltpu.VMEM((span * PAIR, H), BF16), pltpu.VMEM((span * PAIR, H), BF16),
            pltpu.VMEM(((span - 2) * PAIR, BAND), BF16),
            pltpu.VMEM((span * PAIR, H), BF16), pltpu.VMEM((span * PAIR, H), BF16),
        ],
        FWD_MIB,
        "forward",
        units=160,
    )(first, m1, m2, m3, m4, joined, w_own, w_m, w_t, w_mh, w_th)

    r1 = spread(grad_pre, 1)
    r2 = spread(grad_pre, 2)
    kept = [turned, v1, f1, f0, latents, weights]
    g3, g2, turned, v1, f1, f0, latents, weights = call(
        backward_a_kernel,
        [((B, H), BF16), ((PAIR, H), BF16)] + [(k.shape, k.dtype) for k in kept],
        [VMEM] * 12 + [ANY] * 4 + [VMEM],
        [
            pltpu.VMEM((5 * PAIR, H), BF16), pltpu.VMEM((3 * PAIR, H), BF16),
            pltpu.VMEM((3 * PAIR, H), BF16), pltpu.VMEM((3 * PAIR, H), BF16),
        ],
        BWD_MIB,
        "backward_a",
        out_specs=[VMEM] * 2 + [ANY] * len(kept),
        aliases={11 + i: 2 + i for i in range(len(kept))},
        units=60,
    )(grad_pre, r1, r2, swap(r1), swap(r2), first, m1, joined, v3, v2, f2, *kept)

    r1 = spread(g2, 1)
    r2 = spread(g2, 2)
    (results,) = call(
        backward_b_kernel,
        [((4, PAIR, H), BF16)],
        [VMEM] * 13,
        [
            pltpu.VMEM((5 * PAIR, H), BF16), pltpu.VMEM((5 * PAIR, H), BF16),
            pltpu.VMEM((3 * PAIR, H), BF16), pltpu.VMEM((3 * PAIR, H), BF16),
        ],
        BWD_MIB,
        "backward_b",
        units=70,
    )(g2, r1, r2, swap(r1), swap(r2), g3, turned, v1, first, f1, f0, latents, weights)

    results = lax.all_to_all(results, "section", 0, 0, tiled=True)
    latent_result, grad_result = call(
        split_kernel,
        [((4, B, H), BF16)] * 2,
        [ANY],
        [pltpu.SemaphoreType.DMA((2,))],
        4,
        "split",
        out_specs=[HBM] * 2,
    )(results)
    return (latent_result[None], grad_result[None])


def solution(mesh):
    devices = np.asarray(mesh.devices)
    sections, parts = devices.shape
    split = Mesh(devices.reshape(sections, parts // 2, 2), ("section", "chip", "core"))
    dom = ("chip", "core")
    in_specs = (
        P(None, dom, None),
        P(None, dom, None),
        P("section", None, None),
        P("section", None, None),
        P("section", None, None),
        P("section", None),
        P(dom, None, None),
        P(dom),
        P(dom),
    )
    out_specs = (P("section", None, dom, None), P("section", None, dom, None))
    return jax.shard_map(body, mesh=split, in_specs=in_specs, out_specs=out_specs, check_vma=False)
```
